32 devices in a mesh: pipe: 2 (over x), expert: 4 (over y, core), dp: 4 (over z).
Axes of the slice: x: 2, y: 2, z: 4, core: 2. Of those that a mesh axis runs over, the one named last changes fastest.
Arguments:
- carry_forward: bfloat16 [2, 64, 7168], P('pipe', 'expert', 'dp'), may hold values from -6 to 6
- carry_cotangent: bfloat16 [2, 64, 7168], P('pipe', 'expert', 'dp'), may hold values from -6 to 6
- saved_input: bfloat16 [2, 64, 7168], P('pipe', 'expert', 'dp'), may hold values from -6 to 6
- routes_forward: int32 [2, 64, 1], P('pipe', 'expert'), may hold values from 0 to 1; in each aligned block of 16 rows (0 to 15, 16 to 31, ..., all dimensions but the last counted through in order) at most 10 rows name the same one
- gates_forward: bfloat16 [2, 64, 1], P('pipe', 'expert'), may hold values from 0.049804688 to 0.59765625
- routes_backward: int32 [2, 64, 1], P('pipe', 'expert'), may hold values from 0 to 1; in each aligned block of 16 rows (0 to 15, 16 to 31, ..., all dimensions but the last counted through in order) at most 10 rows name the same one
- gates_backward: bfloat16 [2, 64, 1], P('pipe', 'expert'), may hold values from 0.049804688 to 0.59765625
- w_gate: bfloat16 [2, 4, 7168, 512], P('pipe', 'expert', 'dp'), may hold values from -0.0625 to 0.0625
- w_up: bfloat16 [2, 4, 7168, 512], P('pipe', 'expert', 'dp'), may hold values from -0.0625 to 0.0625
- w_down: bfloat16 [2, 4, 512, 7168], P('pipe', 'expert', None, 'dp'), may hold values from -0.1875 to 0.1875
Outputs:
- forward_out: bfloat16 [2, 64, 7168], P('pipe', 'expert', 'dp')
- backward_out: bfloat16 [2, 64, 7168], P('pipe', 'expert', 'dp')
The draws below stay inside these ranges and needn't reach their ends.
Inputs may be any that keep to these rules, and one draw needn't show every extreme that they name: `routes_forward`: within each section, the 16 tokens of one index of expert name any one expert at most 10 times; in some such blocks an expert is named exactly 10 times. A token names 1 different experts. `routes_backward`: as for routes_forward.
All inputs are finite; a program needn't handle non-finite values.
Results may differ from the reference program's by a relative error of at most 0.0032.
Values may be sent and summed in bfloat16 or wider, within the bound.
No kernel may reach another device: no remote copies, remote signals or barrier semaphores. Data moves between devices by JAX's collectives and lax.ppermute only.
A program may use at most 64 MiB of HBM per device.

```python
import math
import jax
import jax.numpy as jnp
import numpy as np
from jax import lax

D = 7168
FF = 1024
TOK_GRP = 16
EXPERTS = 2
TOPK = 1
CAP = 10
TOKENS = 64
N_PIPE = 2
N_EXPERT = 4


def steps_of(rng, shape, split, smallest, largest):
    factor_of = 1.0
    for position, shards_of in split:
        draws = jax.random.uniform(jax.random.fold_in(jax.random.fold_in(rng, 6), position), (shards_of,), jnp.float32, smallest / len(split), largest / len(split))
        factor_of = factor_of * jnp.repeat(jnp.exp(draws), shape[position] // shards_of).reshape((-1,) + (1,) * (len(shape) - 1 - position))
    return factor_of


def routed_block(rng, own, number, rows, number_of, top, reach, skew):
    order = jax.random.permutation(rng, number_of)
    crowded, usual = portions_of(number_of, rows * top, reach, skew, True), portions_of(number_of, rows * top, reach, skew, False)
    places = jnp.arange(number_of)

    def named(tallies, offset_by):
        used = int((tallies > 0).sum())
        fixed = max(1, used // 4)
        moved = fixed + (places - fixed + offset_by * (used - fixed)) % max(1, number_of - fixed)
        return jnp.zeros((number_of,), jnp.int32).at[order[jnp.where(places < fixed, places, moved)]].set(jnp.asarray(tallies, jnp.int32))

    tallies = jnp.where(number % 4 == 0, named(crowded, number // 4), named(usual, number - number // 4 - 1))
    mixed = jax.random.permutation(jax.random.fold_in(own, 3), number_of)
    giver, taker = mixed[0:number_of // 2 * 2:2], mixed[1:number_of // 2 * 2:2]
    slack = jnp.minimum(tallies[giver] - 1, reach - tallies[taker]) // 2
    slack = jnp.where((giver == order[0]) | (taker == order[0]) | (tallies[taker] == 0), 0, jnp.maximum(slack, 0))
    moved = jax.random.randint(jax.random.fold_in(own, 4), (number_of // 2,), 0, 1 << 20) % (slack + 1)
    tallies = tallies.at[giver].add(-moved).at[taker].add(moved)
    labels = jnp.searchsorted(jnp.cumsum(tallies), jnp.arange(rows * top), side="right").astype(jnp.int32)
    listing = labels.reshape(top, rows).T
    listing = listing[jax.random.permutation(jax.random.fold_in(own, 1), rows)]
    offset_by = jax.random.randint(jax.random.fold_in(own, 2), (rows, 1), 0, top)
    return jnp.take_along_axis(listing, (jnp.arange(top)[None, :] + offset_by) % top, axis=1)


def portions_of(number_of, total, most, lean, full):
    loads = [(1 << 20) // math.isqrt(rank ** lean) + 1 for rank in range(1, number_of + 1)]
    largest = most if full else min(most, max(-(-total // number_of), total * loads[0] // sum(loads)))
    least = 1 if total - largest >= number_of - 1 else 0
    counts, rest = [largest] + [least] * (number_of - 1), total - largest - least * (number_of - 1)
    while rest > 0:
        free = [i for i in range(1, number_of) if counts[i] < largest] or [i for i in range(1, number_of) if counts[i] < most]
        mass, left = sum([loads[i] for i in free]), rest
        for i in free:
            more = min(most - counts[i], max(1, left * loads[i] // mass), rest)
            counts[i] = counts[i] + more
            rest = rest - more
    return np.array(counts)


def noise(rng, extent, width, limit, shards=(), held_as=jnp.bfloat16):
    result = width * jax.random.normal(rng, extent, jnp.float32)
    if shards:
        result = result * steps_of(rng, extent, shards, -0.22, 0.18)
    return jnp.clip(result, -limit, limit).astype(held_as)


def setup_inputs(seed: int = 0) -> dict:
    key_of = jax.random.split(jax.random.key(seed), 11)
    carry_forward = noise(key_of[0], (N_PIPE, TOKENS, D), 1.0, 6.0, ((0, 2), (1, 4), (2, 4)))
    carry_cotangent = noise(key_of[1], (N_PIPE, TOKENS, D), 1.0, 6.0, ((0, 2), (1, 4), (2, 4)))
    saved_input = noise(key_of[2], (N_PIPE, TOKENS, D), 1.0, 6.0, ((0, 2), (1, 4), (2, 4)))
    routes_forward_keys = jax.random.split(jax.random.fold_in(key_of[3], 1), N_PIPE * TOKENS // TOK_GRP)
    routes_forward_turns = jax.random.permutation(jax.random.fold_in(key_of[3], 3), N_PIPE * TOKENS // TOK_GRP)
    routes_forward = jax.vmap(lambda own, number: routed_block(jax.random.fold_in(key_of[3], 2), own, number, TOK_GRP, EXPERTS, TOPK, CAP, 2))(routes_forward_keys, routes_forward_turns).reshape((N_PIPE, TOKENS, TOPK))
    gates_forward = jnp.clip(0.049804688 + 0.54785156 * jax.random.uniform(key_of[4], (N_PIPE, TOKENS, TOPK), jnp.float32) ** steps_of(key_of[4], (N_PIPE, TOKENS, TOPK), ((0, 2), (1, 4)), -0.2, 0.2), 0.049804688, 0.59765625).astype(jnp.bfloat16)
    routes_backward_keys = jax.random.split(jax.random.fold_in(key_of[5], 1), N_PIPE * TOKENS // TOK_GRP)
    routes_backward_turns = jax.random.permutation(jax.random.fold_in(key_of[5], 3), N_PIPE * TOKENS // TOK_GRP)
    routes_backward = jax.vmap(lambda own, number: routed_block(jax.random.fold_in(key_of[5], 2), own, number, TOK_GRP, EXPERTS, TOPK, CAP, 2))(routes_backward_keys, routes_backward_turns).reshape((N_PIPE, TOKENS, TOPK))
    gates_backward = jnp.clip(0.049804688 + 0.54785156 * jax.random.uniform(key_of[6], (N_PIPE, TOKENS, TOPK), jnp.float32) ** steps_of(key_of[6], (N_PIPE, TOKENS, TOPK), ((0, 2), (1, 4)), -0.2, 0.2), 0.049804688, 0.59765625).astype(jnp.bfloat16)
    w_gate = noise(key_of[7], (N_PIPE, N_EXPERT, D, FF // 2), D ** -0.5, 0.0625, ((0, 2), (1, 4), (2, 4)))
    w_up = noise(key_of[8], (N_PIPE, N_EXPERT, D, FF // 2), D ** -0.5, 0.0625, ((0, 2), (1, 4), (2, 4)))
    w_down = noise(key_of[9], (N_PIPE, N_EXPERT, FF // 2, D), FF ** -0.5, 0.1875, ((0, 2), (1, 4), (3, 4)))
    return {"carry_forward": carry_forward, "carry_cotangent": carry_cotangent, "saved_input": saved_input, "routes_forward": routes_forward, "gates_forward": gates_forward, "routes_backward": routes_backward, "gates_backward": gates_backward, "w_gate": w_gate, "w_up": w_up, "w_down": w_down}


def tables(routes, gates, experts, capacity):
    kinds = jnp.arange(experts, dtype=jnp.int32)
    onehot = (routes[:, :, None] == kinds).astype(jnp.int32).reshape(-1, experts)
    before = jnp.cumsum(onehot, axis=0) - onehot
    slot = jnp.sum(before * onehot, axis=1).reshape(routes.shape).astype(jnp.int32)
    index = routes * capacity + slot
    columns = jnp.arange(experts * capacity, dtype=jnp.int32)
    hit = index[:, :, None] == columns
    place = jnp.sum(hit.astype(jnp.float32), axis=1).astype(jnp.bfloat16)
    weigh = jnp.sum(jnp.where(hit, gates.astype(jnp.float32)[:, :, None], 0.0), axis=1).astype(jnp.bfloat16)
    return place, weigh


def expert_forward(rows, w_g, w_u, w_d):
    gate = jnp.dot(rows, w_g, preferred_element_type=jnp.float32)
    upper = jnp.dot(rows, w_u, preferred_element_type=jnp.float32)
    hidden = (jax.nn.silu(gate) * upper).astype(jnp.bfloat16)
    return jnp.dot(hidden, w_d, preferred_element_type=jnp.float32).astype(jnp.bfloat16)


def expert_backward(rows, grads, w_g, w_u, w_d):
    gate = jnp.dot(rows, w_g, preferred_element_type=jnp.float32)
    upper = jnp.dot(rows, w_u, preferred_element_type=jnp.float32)
    dhid = jnp.dot(grads, w_d.T, preferred_element_type=jnp.float32)
    sigma = jax.nn.sigmoid(gate)
    active = gate * sigma
    slope = sigma * (1.0 + gate * (1.0 - sigma))
    dgate = (dhid * upper * slope).astype(jnp.bfloat16)
    dupper = (dhid * active).astype(jnp.bfloat16)
    total = jnp.dot(dgate, w_g.T, preferred_element_type=jnp.float32) + jnp.dot(dupper, w_u.T, preferred_element_type=jnp.float32)
    return total.astype(jnp.bfloat16)


def to_devices(table, blocks):
    sent = jnp.einsum("btj,btd->bjd", table.astype(jnp.float32), blocks.astype(jnp.float32)).astype(jnp.bfloat16)
    sent = sent.reshape(N_EXPERT, EXPERTS, CAP, D).transpose(1, 0, 2, 3)
    sent = jnp.repeat(sent, 2, axis=0)
    return sent.reshape(N_EXPERT, N_EXPERT * CAP, D)


def from_devices(rows):
    back = rows.reshape(N_EXPERT, N_EXPERT, CAP, D).transpose(1, 0, 2, 3)
    return back.reshape(N_EXPERT, N_EXPERT * CAP, D)


def widen(table):
    wide = table.reshape(N_EXPERT, TOK_GRP, EXPERTS, CAP)
    return jnp.repeat(wide, 2, axis=2).reshape(N_EXPERT, TOK_GRP, N_EXPERT * CAP)


def reference(carry_forward, carry_cotangent, saved_input, routes_forward, gates_forward, routes_backward, gates_backward, w_gate, w_up, w_down):
    make = jax.vmap(lambda r, g: tables(r, g, EXPERTS, CAP))
    fwd_list = []
    bwd_list = []
    for section in range(N_PIPE):
        prior = (section - 1) % N_PIPE
        xf = carry_forward[prior].reshape(N_EXPERT, TOK_GRP, D)
        cb = carry_cotangent[prior].reshape(N_EXPERT, TOK_GRP, D)
        xb = saved_input[section].reshape(N_EXPERT, TOK_GRP, D)
        place_f, weigh_f = make(routes_forward[section].reshape(N_EXPERT, TOK_GRP, TOPK), gates_forward[section].reshape(N_EXPERT, TOK_GRP, TOPK))
        place_b, weigh_b = make(routes_backward[section].reshape(N_EXPERT, TOK_GRP, TOPK), gates_backward[section].reshape(N_EXPERT, TOK_GRP, TOPK))
        rows_f = to_devices(place_f, xf)
        rows_b = to_devices(place_b, xb)
        grads_b = to_devices(weigh_b, cb)
        outs_f = lax.map(lambda a: expert_forward(*a), (rows_f, w_gate[section], w_up[section], w_down[section]))
        outs_b = lax.map(lambda a: expert_backward(*a), (rows_b, grads_b, w_gate[section], w_up[section], w_down[section]))
        back_f = from_devices(outs_f)
        back_b = from_devices(outs_b)
        result_f = xf.astype(jnp.float32) + jnp.einsum("btj,bjd->btd", widen(weigh_f).astype(jnp.float32), back_f.astype(jnp.float32))
        result_b = cb.astype(jnp.float32) + jnp.einsum("btj,bjd->btd", widen(place_b).astype(jnp.float32), back_b.astype(jnp.float32))
        fwd_list.append(result_f.astype(jnp.bfloat16).reshape(TOKENS, D))
        bwd_list.append(result_b.astype(jnp.bfloat16).reshape(TOKENS, D))
    return jnp.stack(fwd_list), jnp.stack(bwd_list)
```

```python
import functools

import jax
import jax.numpy as jnp
from jax import lax
from jax.experimental import pallas as pl
from jax.experimental.pallas import tpu as pltpu
from jax.sharding import PartitionSpec as P

BF16 = jnp.bfloat16
F32 = jnp.float32
LANES = 128
VMEM_LIMIT = 24 * 1024 * 1024


def in_vmem(x):
    return pltpu.with_memory_space_constraint(x, pltpu.VMEM)


def kernel_call(body, out_shape, flops, bytes_accessed):
    return pl.pallas_call(
        body,
        out_shape=out_shape,
        compiler_params=pltpu.CompilerParams(vmem_limit_bytes=VMEM_LIMIT),
        cost_estimate=pl.CostEstimate(flops=flops, bytes_accessed=bytes_accessed, transcendentals=0),
    )


def swap(x, axis, bit):
    peers = lax.axis_size(axis)
    return lax.ppermute(x, axis, [(i, i ^ bit) for i in range(peers)])


def onward(x, bit):
    sections = lax.axis_size("pipe")
    peers = lax.axis_size("expert")
    pairs = [
        (s * peers + i, (s + 1) % sections * peers + (i ^ bit))
        for s in range(sections)
        for i in range(peers)
    ]
    return lax.ppermute(x, ("pipe", "expert"), pairs)


def pack_kernel(topk, x_ref, c_ref, b_ref, rf_ref, gf_ref, rb_ref, gb_ref, moved_ref, saved_ref):
    rows, width = x_ref.shape
    moved_ref[:rows, :] = x_ref[...]
    moved_ref[rows:, :] = c_ref[...]
    saved_ref[:, :width] = b_ref[...]
    lane = lax.broadcasted_iota(jnp.int32, (rows, LANES), 1)
    notes = jnp.zeros((rows, LANES), F32)
    for group, ref in enumerate((rf_ref, gf_ref, rb_ref, gb_ref)):
        values = ref[...].astype(F32)
        for choice in range(topk):
            notes = jnp.where(lane == group * topk + choice, values[:, choice : choice + 1], notes)
    saved_ref[:, width:] = notes.astype(BF16)


def places(notes, first, topk, expert, rows):
    tokens = notes.shape[1]
    hit = (notes[first : first + topk] == expert).astype(F32)
    named = jnp.sum(hit, axis=0, keepdims=True)
    weight = jnp.sum(hit * notes[first + topk : first + 2 * topk], axis=0, keepdims=True)
    earlier = lax.broadcasted_iota(jnp.int32, (tokens, tokens), 0) < lax.broadcasted_iota(
        jnp.int32, (tokens, tokens), 1
    )
    rank = jnp.dot(
        jnp.broadcast_to(named, (8, tokens)).astype(BF16),
        earlier.astype(BF16),
        preferred_element_type=F32,
    )[:1]
    row = lax.broadcasted_iota(jnp.int32, (rows, tokens), 0).astype(F32)
    place = jnp.where((row == rank) & (named > 0.0), 1.0, 0.0)
    return place, place * weight


def up_kernel(groups, topk, rows, *refs):
    moved = refs[: 2 * groups]
    saved = refs[2 * groups : 4 * groups]
    w_g_ref, w_u_ref, w_d_ref, part_ref, place_f_ref, place_b_ref = refs[4 * groups :]
    held = moved[0].shape[0] // 2
    width = moved[0].shape[1]
    expert = (lax.axis_index("expert") // 2).astype(F32)
    notes = jnp.concatenate([r[:, width:] for r in saved], axis=0).astype(F32).T
    place_f, _ = places(notes, 0, topk, expert, rows)
    place_b, weigh_b = places(notes, 2 * topk, topk, expert, rows)
    place_f_ref[...] = place_f.astype(BF16)
    place_b_ref[...] = place_b.astype(BF16)
    x_f = jnp.concatenate([r[:held, :] for r in moved], axis=0)
    c_b = jnp.concatenate([r[held:, :] for r in moved], axis=0)
    x_b = jnp.concatenate([r[:, :width] for r in saved], axis=0)
    rows_f = jnp.dot(place_f.astype(BF16), x_f, preferred_element_type=F32)
    rows_b = jnp.dot(place_b.astype(BF16), x_b, preferred_element_type=F32)
    grads_b = jnp.dot(weigh_b.astype(BF16), c_b, preferred_element_type=F32).astype(BF16)
    both = jnp.concatenate([rows_f, rows_b], axis=0).astype(BF16)
    gate = jnp.dot(both, w_g_ref[...], preferred_element_type=F32)
    upper = jnp.dot(both, w_u_ref[...], preferred_element_type=F32)
    dhid = lax.dot_general(grads_b, w_d_ref[...], (((1,), (1,)), ((), ())), preferred_element_type=F32)
    part_ref[...] = jnp.concatenate([gate, upper, dhid], axis=0).astype(BF16)


def down_kernel(
    groups, rows, a_ref, b_ref, place_f_ref, place_b_ref, w_g_ref, w_u_ref, w_d_ref, own_ref, other_ref
):
    total = a_ref[...].astype(F32) + b_ref[...].astype(F32)
    gate_f, gate_b, upper_f, upper_b, dhid = [total[i * rows : (i + 1) * rows] for i in range(5)]
    hidden = (gate_f * jax.nn.sigmoid(gate_f) * upper_f).astype(BF16)
    sigma = jax.nn.sigmoid(gate_b)
    slope = sigma * (1.0 + gate_b * (1.0 - sigma))
    dgate = (dhid * upper_b * slope).astype(BF16)
    dupper = (dhid * (gate_b * sigma)).astype(BF16)
    turned = (((1,), (1,)), ((), ()))
    out_f = jnp.dot(hidden, w_d_ref[...], preferred_element_type=F32).astype(BF16)
    grad = lax.dot_general(dgate, w_g_ref[...], turned, preferred_element_type=F32)
    grad = grad + lax.dot_general(dupper, w_u_ref[...], turned, preferred_element_type=F32)
    grad = grad.astype(BF16)
    back = (((0,), (0,)), ((), ()))
    full_f = lax.dot_general(place_f_ref[...], out_f, back, preferred_element_type=F32).astype(BF16)
    full_b = lax.dot_general(place_b_ref[...], grad, back, preferred_element_type=F32).astype(BF16)
    held = own_ref.shape[1] // 2
    for d in range(groups):
        for ref, at in ((own_ref, d * held), (other_ref, (groups + d) * held)):
            ref[d, :held, :] = full_f[at : at + held]
            ref[d, held:, :] = full_b[at : at + held]


def final_kernel(groups, moved_ref, rf_ref, gf_ref, own_ref, other_ref, *refs):
    came = refs[: groups - 1]
    out_f_ref, out_b_ref = refs[groups - 1 :]
    held = out_f_ref.shape[0]
    mine = lax.axis_index("expert") // 2
    routes_f = rf_ref[...]
    gates_f = gf_ref[...].astype(F32)
    result_f = moved_ref[:held, :].astype(F32)
    result_b = moved_ref[held:, :].astype(F32)
    for d in range(groups):
        if d == 0:
            halves = own_ref[0].astype(F32) + other_ref[0].astype(F32)
        else:
            halves = came[d - 1][...].astype(F32)
        weight = jnp.sum(jnp.where(routes_f == (mine ^ d), gates_f, 0.0), axis=1, keepdims=True)
        result_f = result_f + weight * halves[:held]
        result_b = result_b + halves[held:]
    out_f_ref[...] = result_f.astype(BF16)
    out_b_ref[...] = result_b.astype(BF16)


def local(
    carry_forward,
    carry_cotangent,
    saved_input,
    routes_forward,
    gates_forward,
    routes_backward,
    gates_backward,
    w_gate,
    w_up,
    w_down,
):
    peers = lax.axis_size("expert")
    experts = peers // 2
    groups = peers // 2
    held, width = carry_forward.shape[1:]
    hidden = w_gate.shape[3]
    topk = routes_forward.shape[2]
    capacity = min(held, max(6, held * topk // experts + 2))
    rows = -(-peers * capacity // 8) * 8
    tokens = peers * held
    w_g = in_vmem(w_gate[0, 0])
    w_u = in_vmem(w_up[0, 0])
    w_d = in_vmem(w_down[0, 0])
    weight_bytes = 6 * width * hidden

    moved, saved = kernel_call(
        functools.partial(pack_kernel, topk),
        (
            jax.ShapeDtypeStruct((2 * held, width), BF16),
            jax.ShapeDtypeStruct((held, width + LANES), BF16),
        ),
        0,
        6 * held * width,
    )(
        carry_forward[0],
        carry_cotangent[0],
        saved_input[0],
        routes_forward[0],
        gates_forward[0],
        routes_backward[0],
        gates_backward[0],
    )
    saved_all = [saved] + [swap(saved, "expert", 2 * d) for d in range(1, groups)]
    moved_all = [onward(moved, 2 * d) for d in range(groups)]
    saved_all = saved_all + [swap(x, "expert", 1) for x in saved_all]
    moved_all = moved_all + [swap(x, "expert", 1) for x in moved_all]
    part, place_f, place_b = kernel_call(
        functools.partial(up_kernel, groups, topk, rows),
        (
            jax.ShapeDtypeStruct((5 * rows, hidden), BF16),
            jax.ShapeDtypeStruct((rows, tokens), BF16),
            jax.ShapeDtypeStruct((rows, tokens), BF16),
        ),
        10 * rows * width * hidden,
        weight_bytes,
    )(*moved_all, *saved_all, w_g, w_u, w_d)
    bit = lax.axis_size("dp") // 2
    while bit > 1:
        part = (part.astype(F32) + swap(part, "dp", bit).astype(F32)).astype(BF16)
        bit //= 2
    other_part = swap(part, "dp", 1)
    own, other = kernel_call(
        functools.partial(down_kernel, groups, rows),
        (
            jax.ShapeDtypeStruct((groups, 2 * held, width), BF16),
            jax.ShapeDtypeStruct((groups, 2 * held, width), BF16),
        ),
        6 * rows * width * hidden,
        weight_bytes,
    )(part, other_part, place_f, place_b, w_g, w_u, w_d)
    other = swap(other, "expert", 1)
    came = []
    for d in range(1, groups):
        halves = (own[d].astype(F32) + other[d].astype(F32)).astype(BF16)
        came.append(swap(halves, "expert", 2 * d))
    result_f, result_b = kernel_call(
        functools.partial(final_kernel, groups),
        (
            jax.ShapeDtypeStruct((held, width), BF16),
            jax.ShapeDtypeStruct((held, width), BF16),
        ),
        0,
        20 * held * width,
    )(moved_all[0], routes_forward[0], gates_forward[0], own, other, *came)
    return (result_f[None], result_b[None])


def solution(mesh):
    placed = (
        P("pipe", "expert", "dp"),
        P("pipe", "expert", "dp"),
        P("pipe", "expert", "dp"),
        P("pipe", "expert", None),
        P("pipe", "expert", None),
        P("pipe", "expert", None),
        P("pipe", "expert", None),
        P("pipe", "expert", "dp", None),
        P("pipe", "expert", "dp", None),
        P("pipe", "expert", None, "dp"),
    )
    return jax.shard_map(
        local,
        mesh=mesh,
        in_specs=placed,
        out_specs=(P("pipe", "expert", "dp"), P("pipe", "expert", "dp")),
        check_vma=False,
    )
```

```python
import functools

import jax
import jax.numpy as jnp
from jax import lax
from jax.experimental import pallas as pl
from jax.experimental.pallas import tpu as pltpu
from jax.sharding import PartitionSpec as P

BF16 = jnp.bfloat16
F32 = jnp.float32
LANES = 128
VMEM_LIMIT = 24 * 1024 * 1024


def in_vmem(x):
    return pltpu.with_memory_space_constraint(x, pltpu.VMEM)


def in_hbm(x):
    return pltpu.with_memory_space_constraint(x, pltpu.HBM)


def kernel_call(body, out_shape, flops, bytes_accessed):
    return pl.pallas_call(
        body,
        out_shape=out_shape,
        compiler_params=pltpu.CompilerParams(vmem_limit_bytes=VMEM_LIMIT),
        cost_estimate=pl.CostEstimate(flops=flops, bytes_accessed=bytes_accessed, transcendentals=0),
    )


def swap(x, axis, bit):
    peers = lax.axis_size(axis)
    return lax.ppermute(x, axis, [(i, i ^ bit) for i in range(peers)])


def onward(x, bit):
    sections = lax.axis_size("pipe")
    peers = lax.axis_size("expert")
    pairs = [
        (s * peers + i, (s + 1) % sections * peers + (i ^ bit))
        for s in range(sections)
        for i in range(peers)
    ]
    return lax.ppermute(x, ("pipe", "expert"), pairs)


def pack_kernel(topk, b_hbm, *refs):
    rows, width = b_hbm.shape
    noted, (saved_ref, *held, sem, sems) = refs[:4], refs[4:]
    copies = [pltpu.make_async_copy(b_hbm, saved_ref.at[:, pl.ds(0, width)], sem)]
    for i, (source, target) in enumerate(zip(noted, held)):
        copies.append(pltpu.make_async_copy(source, target, sems.at[i]))
    for copy in copies:
        copy.start()
    for copy in copies[1:]:
        copy.wait()
    notes = jnp.concatenate([r[...].astype(F32) for r in held], axis=0)
    for first in range(0, saved_ref.shape[1] - width, LANES):
        block = first // LANES * rows
        part = notes[block : block + rows]
        part = jnp.pad(part, ((0, rows - part.shape[0]), (0, LANES - part.shape[1])))
        saved_ref[:, width + first : width + first + LANES] = part.astype(BF16)
    copies[0].wait()


def fetch_kernel(*refs):
    count = len(refs) // 2
    sems = refs[-1]
    copies = [
        pltpu.make_async_copy(refs[i], refs[count + i], sems.at[i]) for i in range(count)
    ]
    for copy in copies:
        copy.start()
    for copy in copies:
        copy.wait()


def unpack(saved, width, held, topk):
    per_tile = LANES // held
    tiles = []
    for first in range(0, len(saved), per_tile):
        tile = None
        for place, ref in enumerate(saved[first : first + per_tile]):
            spare = ref.shape[1] - width
            part = jnp.concatenate(
                [
                    ref[:, width + j * LANES : width + (j + 1) * LANES].astype(F32)
                    for j in range(spare // LANES)
                ],
                axis=0,
            )
            if place:
                part = pltpu.roll(part, place * held, 1)
            tile = part if tile is None else tile + part
        tiles.append(tile)
    notes = jnp.concatenate(tiles, axis=1) if len(tiles) > 1 else tiles[0]
    return notes[:, : len(saved) * held]


def places(notes, first, topk, expert, rows):
    tokens = notes.shape[1]
    hit = (notes[first : first + topk] == expert).astype(F32)
    named = jnp.sum(hit, axis=0, keepdims=True)
    weight = jnp.sum(hit * notes[first + topk : first + 2 * topk], axis=0, keepdims=True)
    earlier = lax.broadcasted_iota(jnp.int32, (tokens, tokens), 0) < lax.broadcasted_iota(
        jnp.int32, (tokens, tokens), 1
    )
    rank = jnp.dot(
        jnp.broadcast_to(named, (8, tokens)).astype(BF16),
        earlier.astype(BF16),
        preferred_element_type=F32,
    )[:1]
    row = lax.broadcasted_iota(jnp.int32, (rows, tokens), 0).astype(F32)
    place = jnp.where((row == rank) & (named > 0.0), 1.0, 0.0)
    return place, place * weight


def up_kernel(groups, topk, rows, *refs):
    moved = refs[: 2 * groups]
    saved = refs[2 * groups : 4 * groups]
    (
        w_g_ref,
        w_u_ref,
        w_d_ref,
        part_f_ref,
        part_b_ref,
        place_f_ref,
        place_b_ref,
    ) = refs[4 * groups :]
    held = moved[0].shape[0] // 2
    width = moved[0].shape[1]
    expert = (lax.axis_index("expert") // 2).astype(F32)
    notes = unpack(saved, width, held, topk)
    place_f, _ = places(notes, 0, topk, expert, rows)
    place_b, weigh_b = places(notes, 2 * topk, topk, expert, rows)
    place_f_ref[...] = place_f.astype(BF16)
    place_b_ref[...] = place_b.astype(BF16)
    x_f = jnp.concatenate([r[:held, :] for r in moved], axis=0)
    c_b = jnp.concatenate([r[held:, :] for r in moved], axis=0)
    x_b = jnp.concatenate([r[:, :width] for r in saved], axis=0)
    rows_f = jnp.dot(place_f.astype(BF16), x_f, preferred_element_type=F32)
    rows_b = jnp.dot(place_b.astype(BF16), x_b, preferred_element_type=F32)
    grads_b = jnp.dot(weigh_b.astype(BF16), c_b, preferred_element_type=F32).astype(BF16)
    both = jnp.concatenate([rows_f, rows_b], axis=0).astype(BF16)
    gate = jnp.dot(both, w_g_ref[...], preferred_element_type=F32)
    upper = jnp.dot(both, w_u_ref[...], preferred_element_type=F32)
    dhid = lax.dot_general(grads_b, w_d_ref[...], (((1,), (1,)), ((), ())), preferred_element_type=F32)
    part_f_ref[...] = jnp.concatenate([gate[:rows], upper[:rows]], axis=0).astype(BF16)
    part_b_ref[...] = jnp.concatenate([gate[rows:], upper[rows:], dhid], axis=0).astype(BF16)


def return_rows(groups, place_ref, out, own_ref, other_ref):
    back = (((0,), (0,)), ((), ()))
    full = lax.dot_general(place_ref[...], out, back, preferred_element_type=F32).astype(BF16)
    held = own_ref.shape[1]
    for d in range(groups):
        own_ref[d] = full[d * held : (d + 1) * held]
        other_ref[d] = full[(groups + d) * held : (groups + d + 1) * held]


def down_kernel(groups, rows, a_ref, b_ref, place_ref, w_d_ref, own_ref, other_ref):
    total = a_ref[...].astype(F32) + b_ref[...].astype(F32)
    gate, upper = total[:rows], total[rows:]
    hidden = (gate * jax.nn.sigmoid(gate) * upper).astype(BF16)
    out = jnp.dot(hidden, w_d_ref[...], preferred_element_type=F32).astype(BF16)
    return_rows(groups, place_ref, out, own_ref, other_ref)


def grad_kernel(groups, rows, a_ref, b_ref, place_ref, w_g_ref, w_u_ref, own_ref, other_ref):
    total = a_ref[...].astype(F32) + b_ref[...].astype(F32)
    gate, upper, dhid = total[:rows], total[rows : 2 * rows], total[2 * rows :]
    sigma = jax.nn.sigmoid(gate)
    slope = sigma * (1.0 + gate * (1.0 - sigma))
    dgate = (dhid * upper * slope).astype(BF16)
    dupper = (dhid * (gate * sigma)).astype(BF16)
    turned = (((1,), (1,)), ((), ()))
    grad = lax.dot_general(dgate, w_g_ref[...], turned, preferred_element_type=F32)
    grad = grad + lax.dot_general(dupper, w_u_ref[...], turned, preferred_element_type=F32)
    return_rows(groups, place_ref, grad.astype(BF16), own_ref, other_ref)


def final_kernel(groups, moved_ref, rf_ref, gf_ref, *refs):
    parts_f = refs[: groups + 1]
    parts_b = refs[groups + 1 : 2 * groups + 2]
    out_f_ref, out_b_ref = refs[2 * groups + 2 :]
    held = out_f_ref.shape[0]
    mine = lax.axis_index("expert") // 2
    routes_f = rf_ref[...]
    gates_f = gf_ref[...].astype(F32)
    same = lax.broadcasted_iota(jnp.int32, (held, held), 0) == lax.broadcasted_iota(
        jnp.int32, (held, held), 1
    )
    result_f = moved_ref[:held, :].astype(F32)
    result_b = moved_ref[held:, :].astype(F32)
    for i, (part_f, part_b) in enumerate(zip(parts_f, parts_b)):
        d = max(0, i - 1)
        weight = jnp.sum(jnp.where(routes_f == (mine ^ d), gates_f, 0.0), axis=0, keepdims=True)
        weigh = jnp.where(same, weight, 0.0).astype(BF16)
        rows_f = part_f[0] if i < 2 else part_f[...]
        rows_b = part_b[0] if i < 2 else part_b[...]
        result_f = result_f + jnp.dot(weigh, rows_f, preferred_element_type=F32)
        result_b = result_b + rows_b.astype(F32)
    out_f_ref[...] = result_f.astype(BF16)
    out_b_ref[...] = result_b.astype(BF16)


def local(
    carry_forward,
    carry_cotangent,
    saved_input,
    routes_forward,
    gates_forward,
    routes_backward,
    gates_backward,
    w_gate,
    w_up,
    w_down,
):
    peers = lax.axis_size("expert")
    experts = peers // 2
    groups = peers // 2
    held, width = carry_forward.shape[1:]
    hidden = w_gate.shape[3]
    topk = routes_forward.shape[2]
    capacity = min(held, max(6, held * topk // experts + 2))
    rows = -(-peers * capacity // 8) * 8
    tokens = peers * held
    weight_bytes = 6 * width * hidden
    w_g, w_u, w_d = pl.pallas_call(
        fetch_kernel,
        out_shape=[pltpu.VMEM(w.shape[2:], BF16) for w in (w_gate, w_up, w_down)],
        in_specs=[pl.BlockSpec(memory_space=pltpu.HBM)] * 3,
        out_specs=[pl.BlockSpec(memory_space=pltpu.VMEM)] * 3,
        scratch_shapes=[pltpu.SemaphoreType.DMA((3,))],
        compiler_params=pltpu.CompilerParams(vmem_limit_bytes=VMEM_LIMIT),
        cost_estimate=pl.CostEstimate(flops=0, bytes_accessed=2 * weight_bytes, transcendentals=0),
    )(*[in_hbm(w[0, 0]) for w in (w_gate, w_up, w_down)])
    routes_f, gates_f, routes_b, gates_b = [
        jnp.swapaxes(a[0], 0, 1)
        for a in (routes_forward, gates_forward, routes_backward, gates_backward)
    ]
    spare = -(-4 * topk // held) * LANES
    saved = pl.pallas_call(
        functools.partial(pack_kernel, topk),
        out_shape=jax.ShapeDtypeStruct((held, width + spare), BF16),
        in_specs=[pl.BlockSpec(memory_space=pltpu.HBM)] * 5,
        out_specs=pl.BlockSpec(memory_space=pltpu.VMEM),
        scratch_shapes=[pltpu.VMEM(a.shape, a.dtype) for a in (routes_f, gates_f, routes_b, gates_b)]
        + [pltpu.SemaphoreType.DMA, pltpu.SemaphoreType.DMA((4,))],
        compiler_params=pltpu.CompilerParams(vmem_limit_bytes=VMEM_LIMIT),
        cost_estimate=pl.CostEstimate(flops=0, bytes_accessed=4 * held * width, transcendentals=0),
    )(*[in_hbm(a) for a in (saved_input[0], routes_f, gates_f, routes_b, gates_b)])
    saved_all = [saved] + [swap(saved, "expert", 2 * d) for d in range(1, groups)]
    moved = jnp.concatenate((carry_forward[0], carry_cotangent[0]), axis=0)
    moved_all = [onward(moved, 2 * d) for d in range(groups)]
    moved_all[0], w_g, w_u, w_d = lax.optimization_barrier((moved_all[0], w_g, w_u, w_d))
    moved_all[1], w_g = lax.optimization_barrier((moved_all[1], w_g))
    w_g, w_u, w_d = in_vmem(w_g), in_vmem(w_u), in_vmem(w_d)
    saved_all = saved_all + [swap(x, "expert", 1) for x in saved_all]
    moved_all = moved_all + [swap(x, "expert", 1) for x in moved_all]
    part_f, part_b, place_f, place_b = kernel_call(
        functools.partial(up_kernel, groups, topk, rows),
        (
            jax.ShapeDtypeStruct((2 * rows, hidden), BF16),
            jax.ShapeDtypeStruct((3 * rows, hidden), BF16),
            jax.ShapeDtypeStruct((rows, tokens), BF16),
            jax.ShapeDtypeStruct((rows, tokens), BF16),
        ),
        10 * rows * width * hidden,
        weight_bytes,
    )(*moved_all, *saved_all, w_g, w_u, w_d)
    returned = [jax.ShapeDtypeStruct((groups, held, width), BF16)] * 2

    def summed(part):
        bit = lax.axis_size("dp") // 2
        while bit > 1:
            part = (part.astype(F32) + swap(part, "dp", bit).astype(F32)).astype(BF16)
            bit //= 2
        return part, swap(part, "dp", 1)

    def brought(own, other):
        other = swap(other, "expert", 1)
        came = []
        for d in range(1, groups):
            halves = (own[d].astype(F32) + other[d].astype(F32)).astype(BF16)
            came.append(swap(halves, "expert", 2 * d))
        return [own, other] + came

    back_b = kernel_call(
        functools.partial(grad_kernel, groups, rows),
        returned,
        4 * rows * width * hidden,
        4 * width * hidden,
    )(*summed(part_b), place_b, w_g, w_u)
    back_f = kernel_call(
        functools.partial(down_kernel, groups, rows),
        returned,
        2 * rows * width * hidden,
        2 * width * hidden,
    )(*summed(part_f), place_f, w_d)
    result_f, result_b = kernel_call(
        functools.partial(final_kernel, groups),
        (
            jax.ShapeDtypeStruct((held, width), BF16),
            jax.ShapeDtypeStruct((held, width), BF16),
        ),
        0,
        20 * held * width,
    )(moved_all[0], routes_f, gates_f, *brought(*back_f), *brought(*back_b))
    return (result_f[None], result_b[None])


def solution(mesh):
    placed = (
        P("pipe", "expert", "dp"),
        P("pipe", "expert", "dp"),
        P("pipe", "expert", "dp"),
        P("pipe", "expert", None),
        P("pipe", "expert", None),
        P("pipe", "expert", None),
        P("pipe", "expert", None),
        P("pipe", "expert", "dp", None),
        P("pipe", "expert", "dp", None),
        P("pipe", "expert", None, "dp"),
    )
    return jax.shard_map(
        local,
        mesh=mesh,
        in_specs=placed,
        out_specs=(P("pipe", "expert", "dp"), P("pipe", "expert", "dp")),
        check_vma=False,
    )
```

```python
import functools

import jax
import jax.numpy as jnp
from jax import lax
from jax.experimental import pallas as pl
from jax.experimental.pallas import tpu as pltpu
from jax.sharding import PartitionSpec as P

BF16 = jnp.bfloat16
F32 = jnp.float32
LANES = 128
VMEM_LIMIT = 24 * 1024 * 1024


def in_vmem(x):
    return pltpu.with_memory_space_constraint(x, pltpu.VMEM)


def in_hbm(x):
    return pltpu.with_memory_space_constraint(x, pltpu.HBM)


def kernel_call(body, out_shape, flops, bytes_accessed):
    return pl.pallas_call(
        body,
        out_shape=out_shape,
        compiler_params=pltpu.CompilerParams(vmem_limit_bytes=VMEM_LIMIT),
        cost_estimate=pl.CostEstimate(flops=flops, bytes_accessed=bytes_accessed, transcendentals=0),
    )


def swap(x, axis, bit):
    peers = lax.axis_size(axis)
    return lax.ppermute(x, axis, [(i, i ^ bit) for i in range(peers)])


def onward(x, bit):
    sections = lax.axis_size("pipe")
    peers = lax.axis_size("expert")
    pairs = [
        (s * peers + i, (s + 1) % sections * peers + (i ^ bit))
        for s in range(sections)
        for i in range(peers)
    ]
    return lax.ppermute(x, ("pipe", "expert"), pairs)


def pack_kernel(x_hbm, c_hbm, b_hbm, *refs):
    rows, width = b_hbm.shape
    noted, (moved_ref, saved_ref, *held, sems) = refs[:4], refs[4:]
    pairs = list(zip(noted, held)) + [
        (x_hbm, moved_ref.at[pl.ds(0, rows)]),
        (c_hbm, moved_ref.at[pl.ds(rows, rows)]),
        (b_hbm, saved_ref.at[:, pl.ds(0, width)]),
    ]
    copies = [
        pltpu.make_async_copy(source, target, sems.at[i]) for i, (source, target) in enumerate(pairs)
    ]
    for copy in copies:
        copy.start()
    for copy in copies[:4]:
        copy.wait()
    notes = jnp.concatenate([r[...].astype(F32) for r in held], axis=0)
    for first in range(0, saved_ref.shape[1] - width, LANES):
        block = first // LANES * rows
        part = notes[block : block + rows]
        part = jnp.pad(part, ((0, rows - part.shape[0]), (0, LANES - part.shape[1])))
        saved_ref[:, width + first : width + first + LANES] = part.astype(BF16)
    for copy in copies[4:]:
        copy.wait()


def fetch_kernel(*refs):
    count = len(refs) // 2
    sems = refs[-1]
    copies = [
        pltpu.make_async_copy(refs[i], refs[count + i], sems.at[i]) for i in range(count)
    ]
    for copy in copies:
        copy.start()
    for copy in copies:
        copy.wait()


def unpack(saved, width, held, topk):
    per_tile = LANES // held
    tiles = []
    for first in range(0, len(saved), per_tile):
        tile = None
        for place, ref in enumerate(saved[first : first + per_tile]):
            spare = ref.shape[1] - width
            part = jnp.concatenate(
                [
                    ref[:, width + j * LANES : width + (j + 1) * LANES].astype(F32)
                    for j in range(spare // LANES)
                ],
                axis=0,
            )
            if place:
                part = pltpu.roll(part, place * held, 1)
            tile = part if tile is None else tile + part
        tiles.append(tile)
    notes = jnp.concatenate(tiles, axis=1) if len(tiles) > 1 else tiles[0]
    return notes[:, : len(saved) * held]


def places(notes, first, topk, expert, rows):
    tokens = notes.shape[1]
    hit = (notes[first : first + topk] == expert).astype(F32)
    named = jnp.sum(hit, axis=0, keepdims=True)
    weight = jnp.sum(hit * notes[first + topk : first + 2 * topk], axis=0, keepdims=True)
    earlier = lax.broadcasted_iota(jnp.int32, (tokens, tokens), 0) < lax.broadcasted_iota(
        jnp.int32, (tokens, tokens), 1
    )
    rank = jnp.dot(
        jnp.broadcast_to(named, (8, tokens)).astype(BF16),
        earlier.astype(BF16),
        preferred_element_type=F32,
    )[:1]
    row = lax.broadcasted_iota(jnp.int32, (rows, tokens), 0).astype(F32)
    place = jnp.where((row == rank) & (named > 0.0), 1.0, 0.0)
    return place, place * weight


def up_kernel(groups, topk, rows, *refs):
    moved = refs[: 2 * groups]
    saved = refs[2 * groups : 4 * groups]
    (
        w_g_ref,
        w_u_ref,
        w_d_ref,
        part_f_ref,
        part_b_ref,
        place_f_ref,
        place_b_ref,
    ) = refs[4 * groups :]
    held = moved[0].shape[0] // 2
    width = moved[0].shape[1]
    expert = (lax.axis_index("expert") // 2).astype(F32)
    notes = unpack(saved, width, held, topk)
    place_f, _ = places(notes, 0, topk, expert, rows)
    place_b, weigh_b = places(notes, 2 * topk, topk, expert, rows)
    place_f_ref[...] = place_f.astype(BF16)
    place_b_ref[...] = place_b.astype(BF16)
    x_f = jnp.concatenate([r[:held, :] for r in moved], axis=0)
    c_b = jnp.concatenate([r[held:, :] for r in moved], axis=0)
    x_b = jnp.concatenate([r[:, :width] for r in saved], axis=0)
    rows_f = jnp.dot(place_f.astype(BF16), x_f, preferred_element_type=F32)
    rows_b = jnp.dot(place_b.astype(BF16), x_b, preferred_element_type=F32)
    grads_b = jnp.dot(weigh_b.astype(BF16), c_b, preferred_element_type=F32).astype(BF16)
    both = jnp.concatenate([rows_f, rows_b], axis=0).astype(BF16)
    gate = jnp.dot(both, w_g_ref[...], preferred_element_type=F32)
    upper = jnp.dot(both, w_u_ref[...], preferred_element_type=F32)
    dhid = lax.dot_general(grads_b, w_d_ref[...], (((1,), (1,)), ((), ())), preferred_element_type=F32)
    part_f_ref[...] = jnp.concatenate([gate[:rows], upper[:rows], dhid], axis=0).astype(BF16)
    part_b_ref[...] = jnp.concatenate([gate[rows:], upper[rows:]], axis=0).astype(BF16)


def down_kernel(
    groups,
    rows,
    fa_ref,
    fb_ref,
    ba_ref,
    bb_ref,
    place_f_ref,
    place_b_ref,
    w_g_ref,
    w_u_ref,
    w_d_ref,
    own_ref,
    other_ref,
):
    total_f = fa_ref[...].astype(F32) + fb_ref[...].astype(F32)
    total_b = ba_ref[...].astype(F32) + bb_ref[...].astype(F32)
    gate_f, upper_f, dhid = [total_f[i * rows : (i + 1) * rows] for i in range(3)]
    gate_b, upper_b = total_b[:rows], total_b[rows:]
    hidden = (gate_f * jax.nn.sigmoid(gate_f) * upper_f).astype(BF16)
    sigma = jax.nn.sigmoid(gate_b)
    slope = sigma * (1.0 + gate_b * (1.0 - sigma))
    dgate = (dhid * upper_b * slope).astype(BF16)
    dupper = (dhid * (gate_b * sigma)).astype(BF16)
    turned = (((1,), (1,)), ((), ()))
    out_f = jnp.dot(hidden, w_d_ref[...], preferred_element_type=F32).astype(BF16)
    grad = lax.dot_general(dgate, w_g_ref[...], turned, preferred_element_type=F32)
    grad = grad + lax.dot_general(dupper, w_u_ref[...], turned, preferred_element_type=F32)
    grad = grad.astype(BF16)
    back = (((0,), (0,)), ((), ()))
    full_f = lax.dot_general(place_f_ref[...], out_f, back, preferred_element_type=F32).astype(BF16)
    full_b = lax.dot_general(place_b_ref[...], grad, back, preferred_element_type=F32).astype(BF16)
    held = own_ref.shape[1] // 2
    for d in range(groups):
        for ref, at in ((own_ref, d * held), (other_ref, (groups + d) * held)):
            ref[d, :held, :] = full_f[at : at + held]
            ref[d, held:, :] = full_b[at : at + held]


def final_kernel(groups, moved_ref, rf_ref, gf_ref, own_ref, other_ref, *refs):
    came = refs[: groups - 1]
    out_f_ref, out_b_ref = refs[groups - 1 :]
    held = out_f_ref.shape[0]
    mine = lax.axis_index("expert") // 2
    routes_f = rf_ref[...]
    gates_f = gf_ref[...].astype(F32)
    same = lax.broadcasted_iota(jnp.int32, (held, held), 0) == lax.broadcasted_iota(
        jnp.int32, (held, held), 1
    )
    result_f = moved_ref[:held, :].astype(F32)
    result_b = moved_ref[held:, :].astype(F32)
    for d in range(groups):
        weight = jnp.sum(jnp.where(routes_f == (mine ^ d), gates_f, 0.0), axis=0, keepdims=True)
        weigh = jnp.where(same, weight, 0.0).astype(BF16)
        for ref in (own_ref.at[0], other_ref.at[0]) if d == 0 else (came[d - 1],):
            result_f = result_f + jnp.dot(weigh, ref[:held, :], preferred_element_type=F32)
            result_b = result_b + ref[held:, :].astype(F32)
    out_f_ref[...] = result_f.astype(BF16)
    out_b_ref[...] = result_b.astype(BF16)


def local(
    carry_forward,
    carry_cotangent,
    saved_input,
    routes_forward,
    gates_forward,
    routes_backward,
    gates_backward,
    w_gate,
    w_up,
    w_down,
):
    peers = lax.axis_size("expert")
    experts = peers // 2
    groups = peers // 2
    held, width = carry_forward.shape[1:]
    hidden = w_gate.shape[3]
    topk = routes_forward.shape[2]
    capacity = min(held, max(6, held * topk // experts + 2))
    rows = -(-peers * capacity // 8) * 8
    tokens = peers * held
    weight_bytes = 6 * width * hidden
    w_g, w_u, w_d = pl.pallas_call(
        fetch_kernel,
        out_shape=[pltpu.VMEM(w.shape[2:], BF16) for w in (w_gate, w_up, w_down)],
        in_specs=[pl.BlockSpec(memory_space=pltpu.HBM)] * 3,
        out_specs=[pl.BlockSpec(memory_space=pltpu.VMEM)] * 3,
        scratch_shapes=[pltpu.SemaphoreType.DMA((3,))],
        compiler_params=pltpu.CompilerParams(vmem_limit_bytes=VMEM_LIMIT),
        cost_estimate=pl.CostEstimate(flops=0, bytes_accessed=2 * weight_bytes, transcendentals=0),
    )(*[in_hbm(w[0, 0]) for w in (w_gate, w_up, w_down)])
    routes_f, gates_f, routes_b, gates_b = [
        jnp.swapaxes(a[0], 0, 1)
        for a in (routes_forward, gates_forward, routes_backward, gates_backward)
    ]
    spare = -(-4 * topk // held) * LANES
    moved, saved = pl.pallas_call(
        pack_kernel,
        out_shape=[
            jax.ShapeDtypeStruct((2 * held, width), BF16),
            jax.ShapeDtypeStruct((held, width + spare), BF16),
        ],
        in_specs=[pl.BlockSpec(memory_space=pltpu.HBM)] * 7,
        out_specs=[pl.BlockSpec(memory_space=pltpu.VMEM)] * 2,
        scratch_shapes=[pltpu.VMEM(a.shape, a.dtype) for a in (routes_f, gates_f, routes_b, gates_b)]
        + [pltpu.SemaphoreType.DMA((7,))],
        compiler_params=pltpu.CompilerParams(vmem_limit_bytes=VMEM_LIMIT),
        cost_estimate=pl.CostEstimate(flops=0, bytes_accessed=12 * held * width, transcendentals=0),
    )(
        *[in_hbm(a[0]) for a in (carry_forward, carry_cotangent, saved_input)],
        *[in_hbm(a) for a in (routes_f, gates_f, routes_b, gates_b)],
    )
    moved_all = [onward(moved, 2 * d) for d in range(groups)]
    moved_all = [onward(moved, 2 * d) for d in range(groups)]
    saved_all = [saved] + [swap(saved, "expert", 2 * d) for d in range(1, groups)]
    saved_all = saved_all + [swap(x, "expert", 1) for x in saved_all]
    moved_all[0], w_g, w_u, w_d = lax.optimization_barrier((moved_all[0], w_g, w_u, w_d))
    moved_all[1], w_g = lax.optimization_barrier((moved_all[1], w_g))
    w_g, w_u, w_d = in_vmem(w_g), in_vmem(w_u), in_vmem(w_d)
    moved_all[0], *saved_all = lax.optimization_barrier((moved_all[0], *saved_all))
    moved_all = moved_all + [swap(x, "expert", 1) for x in moved_all]
    part_f, part_b, place_f, place_b = kernel_call(
        functools.partial(up_kernel, groups, topk, rows),
        (
            jax.ShapeDtypeStruct((3 * rows, hidden), BF16),
            jax.ShapeDtypeStruct((2 * rows, hidden), BF16),
            jax.ShapeDtypeStruct((rows, tokens), BF16),
            jax.ShapeDtypeStruct((rows, tokens), BF16),
        ),
        10 * rows * width * hidden,
        weight_bytes,
    )(*moved_all, *saved_all, w_g, w_u, w_d)
    bits = [1 << i for i in range(lax.axis_size("dp").bit_length() - 1)]
    last = bits[-1]
    for up, down in zip(bits, bits[::-1]):
        came_f = swap(part_f, "dp", up)
        came_b = swap(part_b, "dp", down)
        if up == last:
            break
        part_f = (part_f.astype(F32) + came_f.astype(F32)).astype(BF16)
        part_b = (part_b.astype(F32) + came_b.astype(F32)).astype(BF16)
    own, other = kernel_call(
        functools.partial(down_kernel, groups, rows),
        [jax.ShapeDtypeStruct((groups, 2 * held, width), BF16)] * 2,
        6 * rows * width * hidden,
        weight_bytes,
    )(part_f, came_f, part_b, came_b, place_f, place_b, w_g, w_u, w_d)
    other = swap(other, "expert", 1)
    came = []
    for d in range(1, groups):
        halves = (own[d].astype(F32) + other[d].astype(F32)).astype(BF16)
        came.append(swap(halves, "expert", 2 * d))
    result_f, result_b = kernel_call(
        functools.partial(final_kernel, groups),
        (
            jax.ShapeDtypeStruct((held, width), BF16),
            jax.ShapeDtypeStruct((held, width), BF16),
        ),
        0,
        20 * held * width,
    )(moved_all[0], routes_f, gates_f, own, other, *came)
    return (result_f[None], result_b[None])


def solution(mesh):
    placed = (
        P("pipe", "expert", "dp"),
        P("pipe", "expert", "dp"),
        P("pipe", "expert", "dp"),
        P("pipe", "expert", None),
        P("pipe", "expert", None),
        P("pipe", "expert", None),
        P("pipe", "expert", None),
        P("pipe", "expert", "dp", None),
        P("pipe", "expert", "dp", None),
        P("pipe", "expert", None, "dp"),
    )
    return jax.shard_map(
        local,
        mesh=mesh,
        in_specs=placed,
        out_specs=(P("pipe", "expert", "dp"), P("pipe", "expert", "dp")),
        check_vma=False,
    )
```

```python
import functools

import jax
import jax.numpy as jnp
from jax import lax
from jax.experimental import pallas as pl
from jax.experimental.pallas import tpu as pltpu
from jax.sharding import PartitionSpec as P

BF16 = jnp.bfloat16
F32 = jnp.float32
LANES = 128
VMEM_LIMIT = 24 * 1024 * 1024


def in_vmem(x):
    return pltpu.with_memory_space_constraint(x, pltpu.VMEM)


def in_hbm(x):
    return pltpu.with_memory_space_constraint(x, pltpu.HBM)


def kernel_call(body, out_shape, flops, bytes_accessed):
    return pl.pallas_call(
        body,
        out_shape=out_shape,
        compiler_params=pltpu.CompilerParams(vmem_limit_bytes=VMEM_LIMIT),
        cost_estimate=pl.CostEstimate(flops=flops, bytes_accessed=bytes_accessed, transcendentals=0),
    )


def swap(x, axis, bit):
    peers = lax.axis_size(axis)
    return lax.ppermute(x, axis, [(i, i ^ bit) for i in range(peers)])


def onward(x, bit):
    sections = lax.axis_size("pipe")
    peers = lax.axis_size("expert")
    pairs = [
        (s * peers + i, (s + 1) % sections * peers + (i ^ bit))
        for s in range(sections)
        for i in range(peers)
    ]
    return lax.ppermute(x, ("pipe", "expert"), pairs)


def pack_kernel(x_hbm, c_hbm, b_hbm, *refs):
    rows, width = b_hbm.shape
    noted, (moved_ref, saved_ref, *held, sems) = refs[:4], refs[4:]
    pairs = list(zip(noted, held)) + [
        (x_hbm, moved_ref.at[pl.ds(0, rows)]),
        (c_hbm, moved_ref.at[pl.ds(rows, rows)]),
        (b_hbm, saved_ref.at[:, pl.ds(0, width)]),
    ]
    copies = [
        pltpu.make_async_copy(source, target, sems.at[i]) for i, (source, target) in enumerate(pairs)
    ]
    for copy in copies:
        copy.start()
    for copy in copies[:4]:
        copy.wait()
    notes = jnp.concatenate([r[...].astype(F32) for r in held], axis=0)
    for first in range(0, saved_ref.shape[1] - width, LANES):
        block = first // LANES * rows
        part = notes[block : block + rows]
        part = jnp.pad(part, ((0, rows - part.shape[0]), (0, LANES - part.shape[1])))
        saved_ref[:, width + first : width + first + LANES] = part.astype(BF16)
    for copy in copies[4:]:
        copy.wait()


def fetch_kernel(*refs):
    count = len(refs) // 2
    sems = refs[-1]
    copies = [
        pltpu.make_async_copy(refs[i], refs[count + i], sems.at[i]) for i in range(count)
    ]
    for copy in copies:
        copy.start()
    for copy in copies:
        copy.wait()


def unpack(saved, width, held, topk):
    per_tile = LANES // held
    tiles = []
    for first in range(0, len(saved), per_tile):
        tile = None
        for place, ref in enumerate(saved[first : first + per_tile]):
            spare = ref.shape[1] - width
            part = jnp.concatenate(
                [
                    ref[:, width + j * LANES : width + (j + 1) * LANES].astype(F32)
                    for j in range(spare // LANES)
                ],
                axis=0,
            )
            if place:
                part = pltpu.roll(part, place * held, 1)
            tile = part if tile is None else tile + part
        tiles.append(tile)
    notes = jnp.concatenate(tiles, axis=1) if len(tiles) > 1 else tiles[0]
    return notes[:, : len(saved) * held]


def places(notes, first, topk, expert, rows, base=0):
    tokens = notes.shape[1]
    hit = (notes[first : first + topk] == expert).astype(F32)
    named = jnp.sum(hit, axis=0, keepdims=True)
    weight = jnp.sum(hit * notes[first + topk : first + 2 * topk], axis=0, keepdims=True)
    earlier = lax.broadcasted_iota(jnp.int32, (tokens, tokens), 0) < lax.broadcasted_iota(
        jnp.int32, (tokens, tokens), 1
    )
    rank = jnp.dot(
        jnp.broadcast_to(named, (8, tokens)).astype(BF16),
        earlier.astype(BF16),
        preferred_element_type=F32,
    )[:1]
    row = lax.broadcasted_iota(jnp.int32, (rows, tokens), 0).astype(F32)
    place = jnp.where((row == rank + base) & (named > 0.0), 1.0, 0.0)
    return place, place * weight, named


def slots(named_f, named_b, held, capacity, slot_rows, rows):
    tokens = named_f.shape[1]
    total = tokens // held * slot_rows
    block = lax.broadcasted_iota(jnp.int32, (total, tokens), 0) // slot_rows
    before = lax.broadcasted_iota(jnp.int32, (total, tokens), 1) < block * held
    offset_f = jnp.sum(jnp.where(before, named_f, 0.0), axis=1, keepdims=True)
    offset_b = jnp.sum(jnp.where(before, named_b, 0.0), axis=1, keepdims=True)
    slot = lax.broadcasted_iota(jnp.int32, (total, 2 * rows), 0) % slot_rows
    row = lax.broadcasted_iota(jnp.int32, (total, 2 * rows), 1)
    slot_value, row_value = slot.astype(F32), row.astype(F32)
    taken_f = (slot < capacity) & (row < rows) & (row_value == offset_f + slot_value)
    taken_b = (
        (slot >= capacity)
        & (slot < 2 * capacity)
        & (row_value == offset_b + slot_value + float(rows - capacity))
    )
    return jnp.where(taken_f | taken_b, 1.0, 0.0)


def home_kernel(topk, capacity, rf_ref, gf_ref, rb_ref, gb_ref, home_ref):
    notes = jnp.concatenate(
        [r[...].astype(F32) for r in (rf_ref, gf_ref, rb_ref, gb_ref)], axis=0
    )
    groups, _, slot_rows = home_ref.shape
    mine = lax.axis_index("expert") // 2
    for d in range(groups):
        expert = (mine ^ d).astype(F32)
        _, weighed, _ = places(notes, 0, topk, expert, slot_rows)
        placed, _, _ = places(notes, 2 * topk, topk, expert, slot_rows, capacity)
        home_ref[d] = jnp.concatenate([weighed, placed], axis=1).T.astype(BF16)


def up_kernel(groups, topk, rows, capacity, slot_rows, *refs):
    moved = refs[: 2 * groups]
    saved = refs[2 * groups : 4 * groups]
    (
        w_g_ref,
        w_u_ref,
        w_d_ref,
        part_f_ref,
        part_b_ref,
        slot_ref,
    ) = refs[4 * groups :]
    held = moved[0].shape[0] // 2
    width = moved[0].shape[1]
    expert = (lax.axis_index("expert") // 2).astype(F32)
    notes = unpack(saved, width, held, topk)
    place_f, _, named_f = places(notes, 0, topk, expert, rows)
    place_b, weigh_b, named_b = places(notes, 2 * topk, topk, expert, rows)
    slot_ref[...] = slots(named_f, named_b, held, capacity, slot_rows, rows).astype(BF16)
    x_f = jnp.concatenate([r[:held, :] for r in moved], axis=0)
    c_b = jnp.concatenate([r[held:, :] for r in moved], axis=0)
    x_b = jnp.concatenate([r[:, :width] for r in saved], axis=0)
    rows_f = jnp.dot(place_f.astype(BF16), x_f, preferred_element_type=F32)
    rows_b = jnp.dot(place_b.astype(BF16), x_b, preferred_element_type=F32)
    grads_b = jnp.dot(weigh_b.astype(BF16), c_b, preferred_element_type=F32).astype(BF16)
    both = jnp.concatenate([rows_f, rows_b], axis=0).astype(BF16)
    gate = jnp.dot(both, w_g_ref[...], preferred_element_type=F32)
    upper = jnp.dot(both, w_u_ref[...], preferred_element_type=F32)
    dhid = lax.dot_general(grads_b, w_d_ref[...], (((1,), (1,)), ((), ())), preferred_element_type=F32)
    part_f_ref[...] = jnp.concatenate([gate[:rows], upper[:rows], dhid], axis=0).astype(BF16)
    part_b_ref[...] = jnp.concatenate([gate[rows:], upper[rows:]], axis=0).astype(BF16)


def down_kernel(
    groups,
    rows,
    fa_ref,
    fb_ref,
    ba_ref,
    bb_ref,
    slot_ref,
    w_g_ref,
    w_u_ref,
    w_d_ref,
    own_ref,
    other_ref,
):
    total_f = fa_ref[...].astype(F32) + fb_ref[...].astype(F32)
    total_b = ba_ref[...].astype(F32) + bb_ref[...].astype(F32)
    gate_f, upper_f, dhid = [total_f[i * rows : (i + 1) * rows] for i in range(3)]
    gate_b, upper_b = total_b[:rows], total_b[rows:]
    hidden = (gate_f * jax.nn.sigmoid(gate_f) * upper_f).astype(BF16)
    sigma = jax.nn.sigmoid(gate_b)
    slope = sigma * (1.0 + gate_b * (1.0 - sigma))
    dgate = (dhid * upper_b * slope).astype(BF16)
    dupper = (dhid * (gate_b * sigma)).astype(BF16)
    turned = (((1,), (1,)), ((), ()))
    out_f = jnp.dot(hidden, w_d_ref[...], preferred_element_type=F32)
    grad = lax.dot_general(dgate, w_g_ref[...], turned, preferred_element_type=F32)
    grad = grad + lax.dot_general(dupper, w_u_ref[...], turned, preferred_element_type=F32)
    both = jnp.concatenate([out_f, grad], axis=0).astype(BF16)
    full = jnp.dot(slot_ref[...], both, preferred_element_type=F32)
    slot_rows = own_ref.shape[1]
    for d in range(groups):
        for ref, block in ((own_ref, d), (other_ref, groups + d)):
            ref[d] = full[block * slot_rows : (block + 1) * slot_rows].astype(BF16)


def final_kernel(groups, moved_ref, home_ref, own_ref, other_ref, *refs):
    came = refs[: groups - 1]
    out_f_ref, out_b_ref = refs[groups - 1 :]
    held = out_f_ref.shape[0]
    result = moved_ref[...].astype(F32)
    for d in range(groups):
        for part in (own_ref[0], other_ref[0]) if d == 0 else (came[d - 1][...],):
            result = result + jnp.dot(home_ref[d], part, preferred_element_type=F32)
    out_f_ref[...] = result[:held].astype(BF16)
    out_b_ref[...] = result[held:].astype(BF16)


def local(
    carry_forward,
    carry_cotangent,
    saved_input,
    routes_forward,
    gates_forward,
    routes_backward,
    gates_backward,
    w_gate,
    w_up,
    w_down,
):
    peers = lax.axis_size("expert")
    experts = peers // 2
    groups = peers // 2
    held, width = carry_forward.shape[1:]
    hidden = w_gate.shape[3]
    topk = routes_forward.shape[2]
    capacity = min(held, max(6, held * topk // experts + 2))
    rows = -(-peers * capacity // 8) * 8
    slot_rows = -(-2 * capacity // 8) * 8
    weight_bytes = 6 * width * hidden
    w_g, w_u, w_d = pl.pallas_call(
        fetch_kernel,
        out_shape=[pltpu.VMEM(w.shape[2:], BF16) for w in (w_gate, w_up, w_down)],
        in_specs=[pl.BlockSpec(memory_space=pltpu.HBM)] * 3,
        out_specs=[pl.BlockSpec(memory_space=pltpu.VMEM)] * 3,
        scratch_shapes=[pltpu.SemaphoreType.DMA((3,))],
        compiler_params=pltpu.CompilerParams(vmem_limit_bytes=VMEM_LIMIT),
        cost_estimate=pl.CostEstimate(flops=0, bytes_accessed=2 * weight_bytes, transcendentals=0),
    )(*[in_hbm(w[0, 0]) for w in (w_gate, w_up, w_down)])
    routes_f, gates_f, routes_b, gates_b = [
        jnp.swapaxes(a[0], 0, 1)
        for a in (routes_forward, gates_forward, routes_backward, gates_backward)
    ]
    spare = -(-4 * topk // held) * LANES
    moved, saved = pl.pallas_call(
        pack_kernel,
        out_shape=[
            jax.ShapeDtypeStruct((2 * held, width), BF16),
            jax.ShapeDtypeStruct((held, width + spare), BF16),
        ],
        in_specs=[pl.BlockSpec(memory_space=pltpu.HBM)] * 7,
        out_specs=[pl.BlockSpec(memory_space=pltpu.VMEM)] * 2,
        scratch_shapes=[pltpu.VMEM(a.shape, a.dtype) for a in (routes_f, gates_f, routes_b, gates_b)]
        + [pltpu.SemaphoreType.DMA((7,))],
        compiler_params=pltpu.CompilerParams(vmem_limit_bytes=VMEM_LIMIT),
        cost_estimate=pl.CostEstimate(flops=0, bytes_accessed=12 * held * width, transcendentals=0),
    )(
        *[in_hbm(a[0]) for a in (carry_forward, carry_cotangent, saved_input)],
        *[in_hbm(a) for a in (routes_f, gates_f, routes_b, gates_b)],
    )
    moved_all = [onward(moved, 2 * d) for d in range(groups)]
    moved_all = [onward(moved, 2 * d) for d in range(groups)]
    saved_all = [saved] + [swap(saved, "expert", 2 * d) for d in range(1, groups)]
    saved_all = saved_all + [swap(x, "expert", 1) for x in saved_all]
    moved_all[0], w_g, w_u, w_d = lax.optimization_barrier((moved_all[0], w_g, w_u, w_d))
    moved_all[1], w_g = lax.optimization_barrier((moved_all[1], w_g))
    w_g, w_u, w_d = in_vmem(w_g), in_vmem(w_u), in_vmem(w_d)
    moved_all[0], *saved_all = lax.optimization_barrier((moved_all[0], *saved_all))
    moved_all = moved_all + [swap(x, "expert", 1) for x in moved_all]
    part_f, part_b, slot = kernel_call(
        functools.partial(up_kernel, groups, topk, rows, capacity, slot_rows),
        (
            jax.ShapeDtypeStruct((3 * rows, hidden), BF16),
            jax.ShapeDtypeStruct((2 * rows, hidden), BF16),
            jax.ShapeDtypeStruct((peers * slot_rows, 2 * rows), BF16),
        ),
        10 * rows * width * hidden,
        weight_bytes,
    )(*moved_all, *saved_all, w_g, w_u, w_d)
    bits = [1 << i for i in range(lax.axis_size("dp").bit_length() - 1)]
    last = bits[-1]
    for up, down in zip(bits, bits[::-1]):
        came_f = swap(part_f, "dp", up)
        came_b = swap(part_b, "dp", down)
        if up == last:
            break
        part_f = (part_f.astype(F32) + came_f.astype(F32)).astype(BF16)
        part_b = (part_b.astype(F32) + came_b.astype(F32)).astype(BF16)
    own, other = kernel_call(
        functools.partial(down_kernel, groups, rows),
        [jax.ShapeDtypeStruct((groups, slot_rows, width), BF16)] * 2,
        6 * rows * width * hidden,
        weight_bytes,
    )(part_f, came_f, part_b, came_b, slot, w_g, w_u, w_d)
    other = swap(other, "expert", 1)
    came = []
    for d in range(1, groups):
        halves = (own[d].astype(F32) + other[d].astype(F32)).astype(BF16)
        came.append(swap(halves, "expert", 2 * d))
    noted = (routes_f, gates_f, routes_b, gates_b)
    *noted, _ = lax.optimization_barrier((*noted, slot))
    home = kernel_call(
        functools.partial(home_kernel, topk, capacity),
        jax.ShapeDtypeStruct((groups, 2 * held, slot_rows), BF16),
        0,
        8 * groups * slot_rows * held,
    )(*noted)
    result_f, result_b = kernel_call(
        functools.partial(final_kernel, groups),
        (
            jax.ShapeDtypeStruct((held, width), BF16),
            jax.ShapeDtypeStruct((held, width), BF16),
        ),
        0,
        20 * held * width,
    )(moved_all[0], home, own, other, *came)
    return (result_f[None], result_b[None])


def solution(mesh):
    placed = (
        P("pipe", "expert", "dp"),
        P("pipe", "expert", "dp"),
        P("pipe", "expert", "dp"),
        P("pipe", "expert", None),
        P("pipe", "expert", None),
        P("pipe", "expert", None),
        P("pipe", "expert", None),
        P("pipe", "expert", "dp", None),
        P("pipe", "expert", "dp", None),
        P("pipe", "expert", None, "dp"),
    )
    return jax.shard_map(
        local,
        mesh=mesh,
        in_specs=placed,
        out_specs=(P("pipe", "expert", "dp"), P("pipe", "expert", "dp")),
        check_vma=False,
    )
```

```python
import functools

import jax
import jax.numpy as jnp
from jax import lax
from jax.experimental import pallas as pl
from jax.experimental.pallas import tpu as pltpu
from jax.sharding import PartitionSpec as P

BF16 = jnp.bfloat16
F32 = jnp.float32
LANES = 128
VMEM_LIMIT = 24 * 1024 * 1024


def in_vmem(x):
    return pltpu.with_memory_space_constraint(x, pltpu.VMEM)


def in_hbm(x):
    return pltpu.with_memory_space_constraint(x, pltpu.HBM)


def kernel_call(body, out_shape, flops, bytes_accessed):
    return pl.pallas_call(
        body,
        out_shape=out_shape,
        compiler_params=pltpu.CompilerParams(vmem_limit_bytes=VMEM_LIMIT),
        cost_estimate=pl.CostEstimate(flops=flops, bytes_accessed=bytes_accessed, transcendentals=0),
    )


def swap(x, axis, bit):
    peers = lax.axis_size(axis)
    return lax.ppermute(x, axis, [(i, i ^ bit) for i in range(peers)])


def onward(x, bit):
    sections = lax.axis_size("pipe")
    peers = lax.axis_size("expert")
    pairs = [
        (s * peers + i, (s + 1) % sections * peers + (i ^ bit))
        for s in range(sections)
        for i in range(peers)
    ]
    return lax.ppermute(x, ("pipe", "expert"), pairs)


def pack_kernel(x_hbm, c_hbm, b_hbm, *refs):
    rows, width = b_hbm.shape
    noted, (moved_ref, saved_ref, *held, sems) = refs[:4], refs[4:]
    pairs = list(zip(noted, held)) + [
        (x_hbm, moved_ref.at[pl.ds(0, rows)]),
        (c_hbm, moved_ref.at[pl.ds(rows, rows)]),
        (b_hbm, saved_ref.at[:, pl.ds(0, width)]),
    ]
    copies = [
        pltpu.make_async_copy(source, target, sems.at[i]) for i, (source, target) in enumerate(pairs)
    ]
    for copy in copies:
        copy.start()
    for copy in copies[:4]:
        copy.wait()
    notes = jnp.concatenate([r[...].astype(F32) for r in held], axis=0)
    for first in range(0, saved_ref.shape[1] - width, LANES):
        block = first // LANES * rows
        part = notes[block : block + rows]
        part = jnp.pad(part, ((0, rows - part.shape[0]), (0, LANES - part.shape[1])))
        saved_ref[:, width + first : width + first + LANES] = part.astype(BF16)
    for copy in copies[4:]:
        copy.wait()


def fetch_kernel(*refs):
    count = len(refs) // 2
    sems = refs[-1]
    copies = [
        pltpu.make_async_copy(refs[i], refs[count + i], sems.at[i]) for i in range(count)
    ]
    for copy in copies:
        copy.start()
    for copy in copies:
        copy.wait()


def unpack(saved, width, held, topk):
    per_tile = LANES // held
    tiles = []
    for first in range(0, len(saved), per_tile):
        tile = None
        for place, ref in enumerate(saved[first : first + per_tile]):
            spare = ref.shape[1] - width
            part = jnp.concatenate(
                [
                    ref[:, width + j * LANES : width + (j + 1) * LANES].astype(F32)
                    for j in range(spare // LANES)
                ],
                axis=0,
            )
            if place:
                part = pltpu.roll(part, place * held, 1)
            tile = part if tile is None else tile + part
        tiles.append(tile)
    notes = jnp.concatenate(tiles, axis=1) if len(tiles) > 1 else tiles[0]
    return notes[:, : len(saved) * held]


def places(notes, first, topk, expert, rows, base=0):
    tokens = notes.shape[1]
    hit = (notes[first : first + topk] == expert).astype(F32)
    named = jnp.sum(hit, axis=0, keepdims=True)
    weight = jnp.sum(hit * notes[first + topk : first + 2 * topk], axis=0, keepdims=True)
    earlier = lax.broadcasted_iota(jnp.int32, (tokens, tokens), 0) < lax.broadcasted_iota(
        jnp.int32, (tokens, tokens), 1
    )
    rank = jnp.dot(
        jnp.broadcast_to(named, (8, tokens)).astype(BF16),
        earlier.astype(BF16),
        preferred_element_type=F32,
    )[:1]
    row = lax.broadcasted_iota(jnp.int32, (rows, tokens), 0).astype(F32)
    place = jnp.where((row == rank + base) & (named > 0.0), 1.0, 0.0)
    return place, place * weight, named


def slots(named_f, named_b, held, capacity, slot_rows, rows):
    tokens = named_f.shape[1]
    total = tokens // held * slot_rows
    block = lax.broadcasted_iota(jnp.int32, (total, tokens), 0) // slot_rows
    before = lax.broadcasted_iota(jnp.int32, (total, tokens), 1) < block * held
    offset_f = jnp.sum(jnp.where(before, named_f, 0.0), axis=1, keepdims=True)
    offset_b = jnp.sum(jnp.where(before, named_b, 0.0), axis=1, keepdims=True)
    slot = lax.broadcasted_iota(jnp.int32, (total, 2 * rows), 0) % slot_rows
    row = lax.broadcasted_iota(jnp.int32, (total, 2 * rows), 1)
    slot_value, row_value = slot.astype(F32), row.astype(F32)
    taken_f = (slot < capacity) & (row < rows) & (row_value == offset_f + slot_value)
    taken_b = (
        (slot >= capacity)
        & (slot < 2 * capacity)
        & (row_value == offset_b + slot_value + float(rows - capacity))
    )
    return jnp.where(taken_f | taken_b, 1.0, 0.0)


def home_kernel(topk, capacity, rf_ref, gf_ref, rb_ref, gb_ref, home_ref):
    notes = jnp.concatenate(
        [r[...].astype(F32) for r in (rf_ref, gf_ref, rb_ref, gb_ref)], axis=0
    )
    groups, _, slot_rows = home_ref.shape
    mine = lax.axis_index("expert") // 2
    for d in range(groups):
        expert = (mine ^ d).astype(F32)
        _, weighed, _ = places(notes, 0, topk, expert, slot_rows)
        placed, _, _ = places(notes, 2 * topk, topk, expert, slot_rows, capacity)
        home_ref[d] = jnp.concatenate([weighed, placed], axis=1).T.astype(BF16)


def up_kernel(groups, topk, rows, capacity, slot_rows, *refs):
    moved = refs[: 2 * groups]
    saved = refs[2 * groups : 4 * groups]
    (
        w_g_ref,
        w_u_ref,
        w_d_ref,
        part_f_ref,
        part_b_ref,
        slot_ref,
    ) = refs[4 * groups :]
    held = moved[0].shape[0] // 2
    width = moved[0].shape[1]
    expert = (lax.axis_index("expert") // 2).astype(F32)
    notes = unpack(saved, width, held, topk)
    place_f, _, named_f = places(notes, 0, topk, expert, rows)
    place_b, weigh_b, named_b = places(notes, 2 * topk, topk, expert, rows)
    slot_ref[...] = slots(named_f, named_b, held, capacity, slot_rows, rows).astype(BF16)
    x_f = jnp.concatenate([r[:held, :] for r in moved], axis=0)
    c_b = jnp.concatenate([r[held:, :] for r in moved], axis=0)
    x_b = jnp.concatenate([r[:, :width] for r in saved], axis=0)
    rows_f = jnp.dot(place_f.astype(BF16), x_f, preferred_element_type=F32)
    rows_b = jnp.dot(place_b.astype(BF16), x_b, preferred_element_type=F32)
    grads_b = jnp.dot(weigh_b.astype(BF16), c_b, preferred_element_type=F32).astype(BF16)
    both = jnp.concatenate([rows_f, rows_b], axis=0).astype(BF16)
    gate = jnp.dot(both, w_g_ref[...], preferred_element_type=F32)
    upper = jnp.dot(both, w_u_ref[...], preferred_element_type=F32)
    dhid = lax.dot_general(grads_b, w_d_ref[...], (((1,), (1,)), ((), ())), preferred_element_type=F32)
    part_f_ref[...] = jnp.concatenate([gate[:rows], upper[:rows], dhid], axis=0).astype(BF16)
    part_b_ref[...] = jnp.concatenate([gate[rows:], upper[rows:]], axis=0).astype(BF16)


def down_kernel(
    groups,
    rows,
    fa_ref,
    fb_ref,
    ba_ref,
    bb_ref,
    slot_ref,
    w_g_ref,
    w_u_ref,
    w_d_ref,
    own_ref,
    other_ref,
):
    total_f = fa_ref[...].astype(F32) + fb_ref[...].astype(F32)
    total_b = ba_ref[...].astype(F32) + bb_ref[...].astype(F32)
    gate_f, upper_f, dhid = [total_f[i * rows : (i + 1) * rows] for i in range(3)]
    gate_b, upper_b = total_b[:rows], total_b[rows:]
    hidden = (gate_f * jax.nn.sigmoid(gate_f) * upper_f).astype(BF16)
    sigma = jax.nn.sigmoid(gate_b)
    slope = sigma * (1.0 + gate_b * (1.0 - sigma))
    dgate = (dhid * upper_b * slope).astype(BF16)
    dupper = (dhid * (gate_b * sigma)).astype(BF16)
    turned = (((1,), (1,)), ((), ()))
    out_f = jnp.dot(hidden, w_d_ref[...], preferred_element_type=F32)
    grad = lax.dot_general(dgate, w_g_ref[...], turned, preferred_element_type=F32)
    grad = grad + lax.dot_general(dupper, w_u_ref[...], turned, preferred_element_type=F32)
    both = jnp.concatenate([out_f, grad], axis=0).astype(BF16)
    full = jnp.dot(slot_ref[...], both, preferred_element_type=F32)
    slot_rows = own_ref.shape[1]
    for d in range(groups):
        for ref, block in ((own_ref, d), (other_ref, groups + d)):
            ref[d] = full[block * slot_rows : (block + 1) * slot_rows].astype(BF16)


def final_kernel(groups, moved_ref, home_ref, own_ref, other_ref, *refs):
    came = refs[: groups - 1]
    out_f_ref, out_b_ref = refs[groups - 1 :]
    held = out_f_ref.shape[0]
    result = moved_ref[...].astype(F32)
    for d in range(groups):
        for part in (own_ref[0], other_ref[0]) if d == 0 else (came[d - 1][...],):
            result = result + jnp.dot(home_ref[d], part, preferred_element_type=F32)
    out_f_ref[...] = result[:held].astype(BF16)
    out_b_ref[...] = result[held:].astype(BF16)


def local(
    carry_forward,
    carry_cotangent,
    saved_input,
    routes_forward,
    gates_forward,
    routes_backward,
    gates_backward,
    w_gate,
    w_up,
    w_down,
):
    peers = lax.axis_size("expert")
    experts = peers // 2
    groups = peers // 2
    held, width = carry_forward.shape[1:]
    hidden = w_gate.shape[3]
    topk = routes_forward.shape[2]
    capacity = min(held, max(6, held * topk // experts + 2))
    rows = -(-peers * capacity // 8) * 8
    slot_rows = -(-2 * capacity // 8) * 8
    weight_bytes = 6 * width * hidden
    w_g, w_u, w_d = pl.pallas_call(
        fetch_kernel,
        out_shape=[pltpu.VMEM(w.shape[2:], BF16) for w in (w_gate, w_up, w_down)],
        in_specs=[pl.BlockSpec(memory_space=pltpu.HBM)] * 3,
        out_specs=[pl.BlockSpec(memory_space=pltpu.VMEM)] * 3,
        scratch_shapes=[pltpu.SemaphoreType.DMA((3,))],
        compiler_params=pltpu.CompilerParams(vmem_limit_bytes=VMEM_LIMIT),
        cost_estimate=pl.CostEstimate(flops=0, bytes_accessed=2 * weight_bytes, transcendentals=0),
    )(*[in_hbm(w[0, 0]) for w in (w_gate, w_up, w_down)])
    routes_f, gates_f, routes_b, gates_b = [
        jnp.swapaxes(a[0], 0, 1)
        for a in (routes_forward, gates_forward, routes_backward, gates_backward)
    ]
    spare = -(-4 * topk // held) * LANES
    moved, saved = pl.pallas_call(
        pack_kernel,
        out_shape=[
            jax.ShapeDtypeStruct((2 * held, width), BF16),
            jax.ShapeDtypeStruct((held, width + spare), BF16),
        ],
        in_specs=[pl.BlockSpec(memory_space=pltpu.HBM)] * 7,
        out_specs=[pl.BlockSpec(memory_space=pltpu.VMEM)] * 2,
        scratch_shapes=[pltpu.VMEM(a.shape, a.dtype) for a in (routes_f, gates_f, routes_b, gates_b)]
        + [pltpu.SemaphoreType.DMA((7,))],
        compiler_params=pltpu.CompilerParams(vmem_limit_bytes=VMEM_LIMIT),
        cost_estimate=pl.CostEstimate(flops=0, bytes_accessed=12 * held * width, transcendentals=0),
    )(
        *[in_hbm(a[0]) for a in (carry_forward, carry_cotangent, saved_input)],
        *[in_hbm(a) for a in (routes_f, gates_f, routes_b, gates_b)],
    )
    moved_all = [onward(moved, 2 * d) for d in range(groups)]
    moved_all = [onward(moved, 2 * d) for d in range(groups)]
    saved_all = [saved] + [swap(saved, "expert", 2 * d) for d in range(1, groups)]
    saved_all = saved_all + [swap(x, "expert", 1) for x in saved_all]
    moved_all[0], w_g, w_u, w_d = lax.optimization_barrier((moved_all[0], w_g, w_u, w_d))
    moved_all[1], w_g = lax.optimization_barrier((moved_all[1], w_g))
    w_g, w_u, w_d = in_vmem(w_g), in_vmem(w_u), in_vmem(w_d)
    moved_swap = []
    for x in moved_all:
        if moved_swap:
            x, *_ = lax.optimization_barrier((x, moved_swap[-1], *saved_all))
        moved_swap.append(swap(x, "expert", 1))
    moved_all = moved_all + moved_swap
    part_f, part_b, slot = kernel_call(
        functools.partial(up_kernel, groups, topk, rows, capacity, slot_rows),
        (
            jax.ShapeDtypeStruct((3 * rows, hidden), BF16),
            jax.ShapeDtypeStruct((2 * rows, hidden), BF16),
            jax.ShapeDtypeStruct((peers * slot_rows, 2 * rows), BF16),
        ),
        10 * rows * width * hidden,
        weight_bytes,
    )(*moved_all, *saved_all, w_g, w_u, w_d)
    bits = [1 << i for i in range(lax.axis_size("dp").bit_length() - 1)]
    last = bits[-1]
    for up, down in zip(bits, bits[::-1]):
        came_f = swap(part_f, "dp", up)
        came_b = swap(part_b, "dp", down)
        if up == last:
            break
        part_f = (part_f.astype(F32) + came_f.astype(F32)).astype(BF16)
        part_b = (part_b.astype(F32) + came_b.astype(F32)).astype(BF16)
    own, other = kernel_call(
        functools.partial(down_kernel, groups, rows),
        [jax.ShapeDtypeStruct((groups, slot_rows, width), BF16)] * 2,
        6 * rows * width * hidden,
        weight_bytes,
    )(part_f, came_f, part_b, came_b, slot, w_g, w_u, w_d)
    other = swap(other, "expert", 1)
    came = []
    for d in range(1, groups):
        halves = (own[d].astype(F32) + other[d].astype(F32)).astype(BF16)
        came.append(swap(halves, "expert", 2 * d))
    noted = (routes_f, gates_f, routes_b, gates_b)
    *noted, _ = lax.optimization_barrier((*noted, slot))
    home = kernel_call(
        functools.partial(home_kernel, topk, capacity),
        jax.ShapeDtypeStruct((groups, 2 * held, slot_rows), BF16),
        0,
        8 * groups * slot_rows * held,
    )(*noted)
    result_f, result_b = kernel_call(
        functools.partial(final_kernel, groups),
        (
            jax.ShapeDtypeStruct((held, width), BF16),
            jax.ShapeDtypeStruct((held, width), BF16),
        ),
        0,
        20 * held * width,
    )(moved_all[0], home, own, other, *came)
    return (result_f[None], result_b[None])


def solution(mesh):
    placed = (
        P("pipe", "expert", "dp"),
        P("pipe", "expert", "dp"),
        P("pipe", "expert", "dp"),
        P("pipe", "expert", None),
        P("pipe", "expert", None),
        P("pipe", "expert", None),
        P("pipe", "expert", None),
        P("pipe", "expert", "dp", None),
        P("pipe", "expert", "dp", None),
        P("pipe", "expert", None, "dp"),
    )
    return jax.shard_map(
        local,
        mesh=mesh,
        in_specs=placed,
        out_specs=(P("pipe", "expert", "dp"), P("pipe", "expert", "dp")),
        check_vma=False,
    )
```

```python
import functools

import jax
import jax.numpy as jnp
from jax import lax
from jax.experimental import pallas as pl
from jax.experimental.pallas import tpu as pltpu
from jax.sharding import PartitionSpec as P

BF16 = jnp.bfloat16
F32 = jnp.float32
LANES = 128
VMEM_LIMIT = 24 * 1024 * 1024


def in_vmem(x):
    return pltpu.with_memory_space_constraint(x, pltpu.VMEM)


def in_hbm(x):
    return pltpu.with_memory_space_constraint(x, pltpu.HBM)


def kernel_call(body, out_shape, flops, bytes_accessed):
    return pl.pallas_call(
        body,
        out_shape=out_shape,
        compiler_params=pltpu.CompilerParams(vmem_limit_bytes=VMEM_LIMIT),
        cost_estimate=pl.CostEstimate(flops=flops, bytes_accessed=bytes_accessed, transcendentals=0),
    )


def swap(x, axis, bit):
    peers = lax.axis_size(axis)
    return lax.ppermute(x, axis, [(i, i ^ bit) for i in range(peers)])


def onward(x, bit):
    sections = lax.axis_size("pipe")
    peers = lax.axis_size("expert")
    pairs = [
        (s * peers + i, (s + 1) % sections * peers + (i ^ bit))
        for s in range(sections)
        for i in range(peers)
    ]
    return lax.ppermute(x, ("pipe", "expert"), pairs)


def pack_kernel(x_hbm, c_hbm, b_hbm, *refs):
    rows, width = b_hbm.shape
    noted, (moved_ref, saved_ref, *held, sems) = refs[:4], refs[4:]
    pairs = list(zip(noted, held)) + [
        (x_hbm, moved_ref.at[pl.ds(0, rows)]),
        (c_hbm, moved_ref.at[pl.ds(rows, rows)]),
        (b_hbm, saved_ref.at[:, pl.ds(0, width)]),
    ]
    copies = [
        pltpu.make_async_copy(source, target, sems.at[i]) for i, (source, target) in enumerate(pairs)
    ]
    for copy in copies:
        copy.start()
    for copy in copies[:4]:
        copy.wait()
    notes = jnp.concatenate([r[...].astype(F32) for r in held], axis=0)
    for first in range(0, saved_ref.shape[1] - width, LANES):
        block = first // LANES * rows
        part = notes[block : block + rows]
        part = jnp.pad(part, ((0, rows - part.shape[0]), (0, LANES - part.shape[1])))
        saved_ref[:, width + first : width + first + LANES] = part.astype(BF16)
    for copy in copies[4:]:
        copy.wait()


def fetch_kernel(*refs):
    count = len(refs) // 2
    sems = refs[-1]
    copies = [
        pltpu.make_async_copy(refs[i], refs[count + i], sems.at[i]) for i in range(count)
    ]
    for copy in copies:
        copy.start()
    for copy in copies:
        copy.wait()


def unpack(saved, width, held, topk):
    per_tile = LANES // held
    tiles = []
    for first in range(0, len(saved), per_tile):
        tile = None
        for place, ref in enumerate(saved[first : first + per_tile]):
            spare = ref.shape[1] - width
            part = jnp.concatenate(
                [
                    ref[:, width + j * LANES : width + (j + 1) * LANES].astype(F32)
                    for j in range(spare // LANES)
                ],
                axis=0,
            )
            if place:
                part = pltpu.roll(part, place * held, 1)
            tile = part if tile is None else tile + part
        tiles.append(tile)
    notes = jnp.concatenate(tiles, axis=1) if len(tiles) > 1 else tiles[0]
    return notes[:, : len(saved) * held]


def places(notes, first, topk, expert, rows, base=0):
    tokens = notes.shape[1]
    hit = (notes[first : first + topk] == expert).astype(F32)
    named = jnp.sum(hit, axis=0, keepdims=True)
    weight = jnp.sum(hit * notes[first + topk : first + 2 * topk], axis=0, keepdims=True)
    earlier = lax.broadcasted_iota(jnp.int32, (tokens, tokens), 0) < lax.broadcasted_iota(
        jnp.int32, (tokens, tokens), 1
    )
    rank = jnp.dot(
        jnp.broadcast_to(named, (8, tokens)).astype(BF16),
        earlier.astype(BF16),
        preferred_element_type=F32,
    )[:1]
    row = lax.broadcasted_iota(jnp.int32, (rows, tokens), 0).astype(F32)
    place = jnp.where((row == rank + base) & (named > 0.0), 1.0, 0.0)
    return place, place * weight, named


def slots(named_f, named_b, held, capacity, slot_rows, rows):
    tokens = named_f.shape[1]
    total = tokens // held * slot_rows
    block = lax.broadcasted_iota(jnp.int32, (total, tokens), 0) // slot_rows
    before = lax.broadcasted_iota(jnp.int32, (total, tokens), 1) < block * held
    offset_f = jnp.sum(jnp.where(before, named_f, 0.0), axis=1, keepdims=True)
    offset_b = jnp.sum(jnp.where(before, named_b, 0.0), axis=1, keepdims=True)
    slot = lax.broadcasted_iota(jnp.int32, (total, 2 * rows), 0) % slot_rows
    row = lax.broadcasted_iota(jnp.int32, (total, 2 * rows), 1)
    slot_value, row_value = slot.astype(F32), row.astype(F32)
    taken_f = (slot < capacity) & (row < rows) & (row_value == offset_f + slot_value)
    taken_b = (
        (slot >= capacity)
        & (slot < 2 * capacity)
        & (row_value == offset_b + slot_value + float(rows - capacity))
    )
    return jnp.where(taken_f | taken_b, 1.0, 0.0)


def home_kernel(topk, capacity, rf_ref, gf_ref, rb_ref, gb_ref, home_ref):
    notes = jnp.concatenate(
        [r[...].astype(F32) for r in (rf_ref, gf_ref, rb_ref, gb_ref)], axis=0
    )
    groups, _, slot_rows = home_ref.shape
    mine = lax.axis_index("expert") // 2
    for d in range(groups):
        expert = (mine ^ d).astype(F32)
        _, weighed, _ = places(notes, 0, topk, expert, slot_rows)
        placed, _, _ = places(notes, 2 * topk, topk, expert, slot_rows, capacity)
        home_ref[d] = jnp.concatenate([weighed, placed], axis=1).T.astype(BF16)


def up_kernel(groups, topk, rows, capacity, slot_rows, *refs):
    moved = refs[: 2 * groups]
    saved = refs[2 * groups : 4 * groups]
    (
        w_g_ref,
        w_u_ref,
        w_d_ref,
        part_f_ref,
        part_b_ref,
        slot_ref,
    ) = refs[4 * groups :]
    held = moved[0].shape[0] // 2
    width = moved[0].shape[1]
    expert = (lax.axis_index("expert") // 2).astype(F32)
    notes = unpack(saved, width, held, topk)
    place_f, _, named_f = places(notes, 0, topk, expert, rows)
    place_b, weigh_b, named_b = places(notes, 2 * topk, topk, expert, rows)
    slot_ref[...] = slots(named_f, named_b, held, capacity, slot_rows, rows).astype(BF16)
    x_f = jnp.concatenate([r[:held, :] for r in moved], axis=0)
    c_b = jnp.concatenate([r[held:, :] for r in moved], axis=0)
    x_b = jnp.concatenate([r[:, :width] for r in saved], axis=0)
    rows_f = jnp.dot(place_f.astype(BF16), x_f, preferred_element_type=F32)
    rows_b = jnp.dot(place_b.astype(BF16), x_b, preferred_element_type=F32)
    grads_b = jnp.dot(weigh_b.astype(BF16), c_b, preferred_element_type=F32).astype(BF16)
    both = jnp.concatenate([rows_f, rows_b], axis=0).astype(BF16)
    gate = jnp.dot(both, w_g_ref[...], preferred_element_type=F32)
    upper = jnp.dot(both, w_u_ref[...], preferred_element_type=F32)
    dhid = lax.dot_general(grads_b, w_d_ref[...], (((1,), (1,)), ((), ())), preferred_element_type=F32)
    cut = part_f_ref.shape[1] - 2 * dhid.shape[1]
    part_f_ref[...] = jnp.concatenate([gate[:rows], upper[:rows], dhid[:, :cut]], axis=1).astype(BF16)
    part_b_ref[...] = jnp.concatenate([gate[rows:], upper[rows:], dhid[:, cut:]], axis=1).astype(BF16)


def down_kernel(
    groups,
    rows,
    fa_ref,
    fb_ref,
    ba_ref,
    bb_ref,
    slot_ref,
    w_g_ref,
    w_u_ref,
    w_d_ref,
    own_ref,
    other_ref,
):
    total_f = fa_ref[...].astype(F32) + fb_ref[...].astype(F32)
    total_b = ba_ref[...].astype(F32) + bb_ref[...].astype(F32)
    units = w_d_ref.shape[0]
    gate_f, upper_f = total_f[:, :units], total_f[:, units : 2 * units]
    gate_b, upper_b = total_b[:, :units], total_b[:, units : 2 * units]
    dhid = jnp.concatenate([total_f[:, 2 * units :], total_b[:, 2 * units :]], axis=1)
    hidden = (gate_f * jax.nn.sigmoid(gate_f) * upper_f).astype(BF16)
    sigma = jax.nn.sigmoid(gate_b)
    slope = sigma * (1.0 + gate_b * (1.0 - sigma))
    dgate = (dhid * upper_b * slope).astype(BF16)
    dupper = (dhid * (gate_b * sigma)).astype(BF16)
    turned = (((1,), (1,)), ((), ()))
    out_f = jnp.dot(hidden, w_d_ref[...], preferred_element_type=F32)
    grad = lax.dot_general(dgate, w_g_ref[...], turned, preferred_element_type=F32)
    grad = grad + lax.dot_general(dupper, w_u_ref[...], turned, preferred_element_type=F32)
    both = jnp.concatenate([out_f, grad], axis=0).astype(BF16)
    full = jnp.dot(slot_ref[...], both, preferred_element_type=F32)
    slot_rows = own_ref.shape[1]
    for d in range(groups):
        for ref, block in ((own_ref, d), (other_ref, groups + d)):
            ref[d] = full[block * slot_rows : (block + 1) * slot_rows].astype(BF16)


def final_kernel(groups, moved_ref, home_ref, own_ref, other_ref, *refs):
    came = refs[: groups - 1]
    out_f_ref, out_b_ref = refs[groups - 1 :]
    held = out_f_ref.shape[0]
    result = moved_ref[...].astype(F32)
    for d in range(groups):
        for part in (own_ref[0], other_ref[0]) if d == 0 else (came[d - 1][...],):
            result = result + jnp.dot(home_ref[d], part, preferred_element_type=F32)
    out_f_ref[...] = result[:held].astype(BF16)
    out_b_ref[...] = result[held:].astype(BF16)


def local(
    carry_forward,
    carry_cotangent,
    saved_input,
    routes_forward,
    gates_forward,
    routes_backward,
    gates_backward,
    w_gate,
    w_up,
    w_down,
):
    peers = lax.axis_size("expert")
    experts = peers // 2
    groups = peers // 2
    held, width = carry_forward.shape[1:]
    hidden = w_gate.shape[3]
    topk = routes_forward.shape[2]
    capacity = min(held, max(6, held * topk // experts + 2))
    rows = -(-peers * capacity // 8) * 8
    cut = hidden * 3 // 4
    slot_rows = -(-2 * capacity // 8) * 8
    weight_bytes = 6 * width * hidden
    w_g, w_u, w_d = pl.pallas_call(
        fetch_kernel,
        out_shape=[pltpu.VMEM(w.shape[2:], BF16) for w in (w_gate, w_up, w_down)],
        in_specs=[pl.BlockSpec(memory_space=pltpu.HBM)] * 3,
        out_specs=[pl.BlockSpec(memory_space=pltpu.VMEM)] * 3,
        scratch_shapes=[pltpu.SemaphoreType.DMA((3,))],
        compiler_params=pltpu.CompilerParams(vmem_limit_bytes=VMEM_LIMIT),
        cost_estimate=pl.CostEstimate(flops=0, bytes_accessed=2 * weight_bytes, transcendentals=0),
    )(*[in_hbm(w[0, 0]) for w in (w_gate, w_up, w_down)])
    routes_f, gates_f, routes_b, gates_b = [
        jnp.swapaxes(a[0], 0, 1)
        for a in (routes_forward, gates_forward, routes_backward, gates_backward)
    ]
    spare = -(-4 * topk // held) * LANES
    moved, saved = pl.pallas_call(
        pack_kernel,
        out_shape=[
            jax.ShapeDtypeStruct((2 * held, width), BF16),
            jax.ShapeDtypeStruct((held, width + spare), BF16),
        ],
        in_specs=[pl.BlockSpec(memory_space=pltpu.HBM)] * 7,
        out_specs=[pl.BlockSpec(memory_space=pltpu.VMEM)] * 2,
        scratch_shapes=[pltpu.VMEM(a.shape, a.dtype) for a in (routes_f, gates_f, routes_b, gates_b)]
        + [pltpu.SemaphoreType.DMA((7,))],
        compiler_params=pltpu.CompilerParams(vmem_limit_bytes=VMEM_LIMIT),
        cost_estimate=pl.CostEstimate(flops=0, bytes_accessed=12 * held * width, transcendentals=0),
    )(
        *[in_hbm(a[0]) for a in (carry_forward, carry_cotangent, saved_input)],
        *[in_hbm(a) for a in (routes_f, gates_f, routes_b, gates_b)],
    )
    moved_all = [onward(moved, 2 * d) for d in range(groups)]
    moved_all = [onward(moved, 2 * d) for d in range(groups)]
    saved_all = [saved] + [swap(saved, "expert", 2 * d) for d in range(1, groups)]
    saved_all = saved_all + [swap(x, "expert", 1) for x in saved_all]
    moved_all[0], w_g, w_u, w_d = lax.optimization_barrier((moved_all[0], w_g, w_u, w_d))
    moved_all[1], w_g = lax.optimization_barrier((moved_all[1], w_g))
    w_g, w_u, w_d = in_vmem(w_g), in_vmem(w_u), in_vmem(w_d)
    moved_swap = []
    for x in moved_all:
        if moved_swap:
            x, *_ = lax.optimization_barrier((x, moved_swap[-1], *saved_all))
        moved_swap.append(swap(x, "expert", 1))
    moved_all = moved_all + moved_swap
    part_f, part_b, slot = kernel_call(
        functools.partial(up_kernel, groups, topk, rows, capacity, slot_rows),
        (
            jax.ShapeDtypeStruct((rows, 2 * hidden + cut), BF16),
            jax.ShapeDtypeStruct((rows, 3 * hidden - cut), BF16),
            jax.ShapeDtypeStruct((peers * slot_rows, 2 * rows), BF16),
        ),
        10 * rows * width * hidden,
        weight_bytes,
    )(*moved_all, *saved_all, w_g, w_u, w_d)
    bits = [1 << i for i in range(lax.axis_size("dp").bit_length() - 1)]
    last = bits[-1]
    for up, down in zip(bits, bits[::-1]):
        came_f = swap(part_f, "dp", up)
        came_b = swap(part_b, "dp", down)
        if up == last:
            break
        part_f = (part_f.astype(F32) + came_f.astype(F32)).astype(BF16)
        part_b = (part_b.astype(F32) + came_b.astype(F32)).astype(BF16)
    own, other = kernel_call(
        functools.partial(down_kernel, groups, rows),
        [jax.ShapeDtypeStruct((groups, slot_rows, width), BF16)] * 2,
        6 * rows * width * hidden,
        weight_bytes,
    )(part_f, came_f, part_b, came_b, slot, w_g, w_u, w_d)
    other = swap(other, "expert", 1)
    came = []
    for d in range(1, groups):
        halves = (own[d].astype(F32) + other[d].astype(F32)).astype(BF16)
        came.append(swap(halves, "expert", 2 * d))
    noted = (routes_f, gates_f, routes_b, gates_b)
    *noted, _ = lax.optimization_barrier((*noted, slot))
    home = kernel_call(
        functools.partial(home_kernel, topk, capacity),
        jax.ShapeDtypeStruct((groups, 2 * held, slot_rows), BF16),
        0,
        8 * groups * slot_rows * held,
    )(*noted)
    result_f, result_b = kernel_call(
        functools.partial(final_kernel, groups),
        (
            jax.ShapeDtypeStruct((held, width), BF16),
            jax.ShapeDtypeStruct((held, width), BF16),
        ),
        0,
        20 * held * width,
    )(moved_all[0], home, own, other, *came)
    return (result_f[None], result_b[None])


def solution(mesh):
    placed = (
        P("pipe", "expert", "dp"),
        P("pipe", "expert", "dp"),
        P("pipe", "expert", "dp"),
        P("pipe", "expert", None),
        P("pipe", "expert", None),
        P("pipe", "expert", None),
        P("pipe", "expert", None),
        P("pipe", "expert", "dp", None),
        P("pipe", "expert", "dp", None),
        P("pipe", "expert", None, "dp"),
    )
    return jax.shard_map(
        local,
        mesh=mesh,
        in_specs=placed,
        out_specs=(P("pipe", "expert", "dp"), P("pipe", "expert", "dp")),
        check_vma=False,
    )
```

```python
import functools

import jax
import jax.numpy as jnp
from jax import lax
from jax.experimental import pallas as pl
from jax.experimental.pallas import tpu as pltpu
from jax.sharding import PartitionSpec as P

BF16 = jnp.bfloat16
F32 = jnp.float32
LANES = 128
VMEM_LIMIT = 24 * 1024 * 1024


def in_vmem(x):
    return pltpu.with_memory_space_constraint(x, pltpu.VMEM)


def in_hbm(x):
    return pltpu.with_memory_space_constraint(x, pltpu.HBM)


def kernel_call(body, out_shape, flops, bytes_accessed):
    return pl.pallas_call(
        body,
        out_shape=out_shape,
        compiler_params=pltpu.CompilerParams(vmem_limit_bytes=VMEM_LIMIT),
        cost_estimate=pl.CostEstimate(flops=flops, bytes_accessed=bytes_accessed, transcendentals=0),
    )


def swap(x, axis, bit):
    peers = lax.axis_size(axis)
    return lax.ppermute(x, axis, [(i, i ^ bit) for i in range(peers)])


def mixed(x, even, odd):
    peers = lax.axis_size("expert")
    parts = lax.axis_size("dp")
    pairs = [
        (i * parts + k, i * parts + (k ^ (odd if i % 2 else even)))
        for i in range(peers)
        for k in range(parts)
    ]
    return lax.ppermute(x, ("expert", "dp"), pairs)


def onward(x, bit):
    sections = lax.axis_size("pipe")
    peers = lax.axis_size("expert")
    pairs = [
        (s * peers + i, (s + 1) % sections * peers + (i ^ bit))
        for s in range(sections)
        for i in range(peers)
    ]
    return lax.ppermute(x, ("pipe", "expert"), pairs)


def pack_kernel(x_hbm, c_hbm, b_hbm, *refs):
    rows, width = b_hbm.shape
    noted, (moved_ref, saved_ref, *held, sems) = refs[:4], refs[4:]
    pairs = list(zip(noted, held)) + [
        (x_hbm, moved_ref.at[pl.ds(0, rows)]),
        (c_hbm, moved_ref.at[pl.ds(rows, rows)]),
        (b_hbm, saved_ref.at[:, pl.ds(0, width)]),
    ]
    copies = [
        pltpu.make_async_copy(source, target, sems.at[i]) for i, (source, target) in enumerate(pairs)
    ]
    for copy in copies:
        copy.start()
    for copy in copies[:4]:
        copy.wait()
    notes = jnp.concatenate([r[...].astype(F32) for r in held], axis=0)
    for first in range(0, saved_ref.shape[1] - width, LANES):
        block = first // LANES * rows
        part = notes[block : block + rows]
        part = jnp.pad(part, ((0, rows - part.shape[0]), (0, LANES - part.shape[1])))
        saved_ref[:, width + first : width + first + LANES] = part.astype(BF16)
    for copy in copies[4:]:
        copy.wait()


def fetch_kernel(*refs):
    count = len(refs) // 2
    sems = refs[-1]
    copies = [
        pltpu.make_async_copy(refs[i], refs[count + i], sems.at[i]) for i in range(count)
    ]
    for copy in copies:
        copy.start()
    for copy in copies:
        copy.wait()


def unpack(saved, width, held, topk):
    per_tile = LANES // held
    tiles = []
    for first in range(0, len(saved), per_tile):
        tile = None
        for place, ref in enumerate(saved[first : first + per_tile]):
            spare = ref.shape[1] - width
            part = jnp.concatenate(
                [
                    ref[:, width + j * LANES : width + (j + 1) * LANES].astype(F32)
                    for j in range(spare // LANES)
                ],
                axis=0,
            )
            if place:
                part = pltpu.roll(part, place * held, 1)
            tile = part if tile is None else tile + part
        tiles.append(tile)
    notes = jnp.concatenate(tiles, axis=1) if len(tiles) > 1 else tiles[0]
    return notes[:, : len(saved) * held]


def places(notes, first, topk, expert, rows, base=0):
    tokens = notes.shape[1]
    hit = (notes[first : first + topk] == expert).astype(F32)
    named = jnp.sum(hit, axis=0, keepdims=True)
    weight = jnp.sum(hit * notes[first + topk : first + 2 * topk], axis=0, keepdims=True)
    earlier = lax.broadcasted_iota(jnp.int32, (tokens, tokens), 0) < lax.broadcasted_iota(
        jnp.int32, (tokens, tokens), 1
    )
    rank = jnp.dot(
        jnp.broadcast_to(named, (8, tokens)).astype(BF16),
        earlier.astype(BF16),
        preferred_element_type=F32,
    )[:1]
    row = lax.broadcasted_iota(jnp.int32, (rows, tokens), 0).astype(F32)
    place = jnp.where((row == rank + base) & (named > 0.0), 1.0, 0.0)
    return place, place * weight, named


def slots(named_f, named_b, held, capacity, slot_rows, rows):
    tokens = named_f.shape[1]
    total = tokens // held * slot_rows
    block = lax.broadcasted_iota(jnp.int32, (total, tokens), 0) // slot_rows
    before = lax.broadcasted_iota(jnp.int32, (total, tokens), 1) < block * held
    offset_f = jnp.sum(jnp.where(before, named_f, 0.0), axis=1, keepdims=True)
    offset_b = jnp.sum(jnp.where(before, named_b, 0.0), axis=1, keepdims=True)
    slot = lax.broadcasted_iota(jnp.int32, (total, 2 * rows), 0) % slot_rows
    row = lax.broadcasted_iota(jnp.int32, (total, 2 * rows), 1)
    slot_value, row_value = slot.astype(F32), row.astype(F32)
    taken_f = (slot < capacity) & (row < rows) & (row_value == offset_f + slot_value)
    taken_b = (
        (slot >= capacity)
        & (slot < 2 * capacity)
        & (row_value == offset_b + slot_value + float(rows - capacity))
    )
    return jnp.where(taken_f | taken_b, 1.0, 0.0)


def home_kernel(topk, capacity, rf_ref, gf_ref, rb_ref, gb_ref, home_ref):
    notes = jnp.concatenate(
        [r[...].astype(F32) for r in (rf_ref, gf_ref, rb_ref, gb_ref)], axis=0
    )
    groups, _, slot_rows = home_ref.shape
    mine = lax.axis_index("expert") // 2
    for d in range(groups):
        expert = (mine ^ d).astype(F32)
        _, weighed, _ = places(notes, 0, topk, expert, slot_rows)
        placed, _, _ = places(notes, 2 * topk, topk, expert, slot_rows, capacity)
        home_ref[d] = jnp.concatenate([weighed, placed], axis=1).T.astype(BF16)


def up_kernel(groups, topk, rows, capacity, slot_rows, *refs):
    moved = refs[: 2 * groups]
    saved = refs[2 * groups : 4 * groups]
    (
        w_g_ref,
        w_u_ref,
        w_d_ref,
        part_f_ref,
        part_b_ref,
        slot_ref,
    ) = refs[4 * groups :]
    held = moved[0].shape[0] // 2
    width = moved[0].shape[1]
    expert = (lax.axis_index("expert") // 2).astype(F32)
    notes = unpack(saved, width, held, topk)
    place_f, _, named_f = places(notes, 0, topk, expert, rows)
    place_b, weigh_b, named_b = places(notes, 2 * topk, topk, expert, rows)
    slot_ref[...] = slots(named_f, named_b, held, capacity, slot_rows, rows).astype(BF16)
    x_f = jnp.concatenate([r[:held, :] for r in moved], axis=0)
    c_b = jnp.concatenate([r[held:, :] for r in moved], axis=0)
    x_b = jnp.concatenate([r[:, :width] for r in saved], axis=0)
    rows_f = jnp.dot(place_f.astype(BF16), x_f, preferred_element_type=F32)
    rows_b = jnp.dot(place_b.astype(BF16), x_b, preferred_element_type=F32)
    grads_b = jnp.dot(weigh_b.astype(BF16), c_b, preferred_element_type=F32).astype(BF16)
    both = jnp.concatenate([rows_f, rows_b], axis=0).astype(BF16)
    gate = jnp.dot(both, w_g_ref[...], preferred_element_type=F32)
    upper = jnp.dot(both, w_u_ref[...], preferred_element_type=F32)
    dhid = lax.dot_general(grads_b, w_d_ref[...], (((1,), (1,)), ((), ())), preferred_element_type=F32)
    cut = part_f_ref.shape[1] - 2 * dhid.shape[1]
    part_f_ref[...] = jnp.concatenate([gate[:rows], upper[:rows], dhid[:, :cut]], axis=1).astype(BF16)
    part_b_ref[...] = jnp.concatenate([gate[rows:], upper[rows:], dhid[:, cut:]], axis=1).astype(BF16)


def down_kernel(
    groups,
    rows,
    fa_ref,
    fb_ref,
    ba_ref,
    bb_ref,
    slot_ref,
    w_g_ref,
    w_u_ref,
    w_d_ref,
    own_ref,
    other_ref,
):
    total_f = fa_ref[...].astype(F32) + fb_ref[...].astype(F32)
    total_b = ba_ref[...].astype(F32) + bb_ref[...].astype(F32)
    units = w_d_ref.shape[0]
    gate_f, upper_f = total_f[:, :units], total_f[:, units : 2 * units]
    gate_b, upper_b = total_b[:, :units], total_b[:, units : 2 * units]
    dhid = jnp.concatenate([total_f[:, 2 * units :], total_b[:, 2 * units :]], axis=1)
    hidden = (gate_f * jax.nn.sigmoid(gate_f) * upper_f).astype(BF16)
    sigma = jax.nn.sigmoid(gate_b)
    slope = sigma * (1.0 + gate_b * (1.0 - sigma))
    dgate = (dhid * upper_b * slope).astype(BF16)
    dupper = (dhid * (gate_b * sigma)).astype(BF16)
    turned = (((1,), (1,)), ((), ()))
    out_f = jnp.dot(hidden, w_d_ref[...], preferred_element_type=F32)
    grad = lax.dot_general(dgate, w_g_ref[...], turned, preferred_element_type=F32)
    grad = grad + lax.dot_general(dupper, w_u_ref[...], turned, preferred_element_type=F32)
    both = jnp.concatenate([out_f, grad], axis=0).astype(BF16)
    full = jnp.dot(slot_ref[...], both, preferred_element_type=F32)
    slot_rows = own_ref.shape[1]
    for d in range(groups):
        for ref, block in ((own_ref, d), (other_ref, groups + d)):
            ref[d] = full[block * slot_rows : (block + 1) * slot_rows].astype(BF16)


def final_kernel(groups, moved_ref, home_ref, own_ref, other_ref, *refs):
    came = refs[: groups - 1]
    out_f_ref, out_b_ref = refs[groups - 1 :]
    held = out_f_ref.shape[0]
    result = moved_ref[...].astype(F32)
    for d in range(groups):
        for part in (own_ref[0], other_ref[0]) if d == 0 else (came[d - 1][...],):
            result = result + jnp.dot(home_ref[d], part, preferred_element_type=F32)
    out_f_ref[...] = result[:held].astype(BF16)
    out_b_ref[...] = result[held:].astype(BF16)


def local(
    carry_forward,
    carry_cotangent,
    saved_input,
    routes_forward,
    gates_forward,
    routes_backward,
    gates_backward,
    w_gate,
    w_up,
    w_down,
):
    peers = lax.axis_size("expert")
    experts = peers // 2
    groups = peers // 2
    held, width = carry_forward.shape[1:]
    hidden = w_gate.shape[3]
    topk = routes_forward.shape[2]
    capacity = min(held, max(6, held * topk // experts + 2))
    rows = -(-peers * capacity // 8) * 8
    cut = hidden * 2 // 4
    slot_rows = -(-2 * capacity // 8) * 8
    weight_bytes = 6 * width * hidden
    w_g, w_u, w_d = pl.pallas_call(
        fetch_kernel,
        out_shape=[pltpu.VMEM(w.shape[2:], BF16) for w in (w_gate, w_up, w_down)],
        in_specs=[pl.BlockSpec(memory_space=pltpu.HBM)] * 3,
        out_specs=[pl.BlockSpec(memory_space=pltpu.VMEM)] * 3,
        scratch_shapes=[pltpu.SemaphoreType.DMA((3,))],
        compiler_params=pltpu.CompilerParams(vmem_limit_bytes=VMEM_LIMIT),
        cost_estimate=pl.CostEstimate(flops=0, bytes_accessed=2 * weight_bytes, transcendentals=0),
    )(*[in_hbm(w[0, 0]) for w in (w_gate, w_up, w_down)])
    routes_f, gates_f, routes_b, gates_b = [
        jnp.swapaxes(a[0], 0, 1)
        for a in (routes_forward, gates_forward, routes_backward, gates_backward)
    ]
    spare = -(-4 * topk // held) * LANES
    moved, saved = pl.pallas_call(
        pack_kernel,
        out_shape=[
            jax.ShapeDtypeStruct((2 * held, width), BF16),
            jax.ShapeDtypeStruct((held, width + spare), BF16),
        ],
        in_specs=[pl.BlockSpec(memory_space=pltpu.HBM)] * 7,
        out_specs=[pl.BlockSpec(memory_space=pltpu.VMEM)] * 2,
        scratch_shapes=[pltpu.VMEM(a.shape, a.dtype) for a in (routes_f, gates_f, routes_b, gates_b)]
        + [pltpu.SemaphoreType.DMA((7,))],
        compiler_params=pltpu.CompilerParams(vmem_limit_bytes=VMEM_LIMIT),
        cost_estimate=pl.CostEstimate(flops=0, bytes_accessed=12 * held * width, transcendentals=0),
    )(
        *[in_hbm(a[0]) for a in (carry_forward, carry_cotangent, saved_input)],
        *[in_hbm(a) for a in (routes_f, gates_f, routes_b, gates_b)],
    )
    moved_all = [onward(moved, 2 * d) for d in range(groups)]
    moved_all = [onward(moved, 2 * d) for d in range(groups)]
    saved_all = [saved] + [swap(saved, "expert", 2 * d) for d in range(1, groups)]
    saved_all = saved_all + [swap(x, "expert", 1) for x in saved_all]
    moved_all[0], w_g, w_u, w_d = lax.optimization_barrier((moved_all[0], w_g, w_u, w_d))
    moved_all[1], w_g = lax.optimization_barrier((moved_all[1], w_g))
    w_g, w_u, w_d = in_vmem(w_g), in_vmem(w_u), in_vmem(w_d)
    moved_swap = []
    for x in moved_all:
        if moved_swap:
            x, *_ = lax.optimization_barrier((x, moved_swap[-1], *saved_all))
        moved_swap.append(swap(x, "expert", 1))
    moved_all = moved_all + moved_swap
    part_f, part_b, slot = kernel_call(
        functools.partial(up_kernel, groups, topk, rows, capacity, slot_rows),
        (
            jax.ShapeDtypeStruct((rows, 2 * hidden + cut), BF16),
            jax.ShapeDtypeStruct((rows, 3 * hidden - cut), BF16),
            jax.ShapeDtypeStruct((peers * slot_rows, 2 * rows), BF16),
        ),
        10 * rows * width * hidden,
        weight_bytes,
    )(*moved_all, *saved_all, w_g, w_u, w_d)
    bits = [1 << i for i in range(lax.axis_size("dp").bit_length() - 1)]
    last = bits[-1]
    for up, down in zip(bits, bits[::-1]):
        came_f = mixed(part_f, up, down)
        came_b = mixed(part_b, up, down)
        if up == last:
            break
        part_f = (part_f.astype(F32) + came_f.astype(F32)).astype(BF16)
        part_b = (part_b.astype(F32) + came_b.astype(F32)).astype(BF16)
    own, other = kernel_call(
        functools.partial(down_kernel, groups, rows),
        [jax.ShapeDtypeStruct((groups, slot_rows, width), BF16)] * 2,
        6 * rows * width * hidden,
        weight_bytes,
    )(part_f, came_f, part_b, came_b, slot, w_g, w_u, w_d)
    other = swap(other, "expert", 1)
    came = []
    for d in range(1, groups):
        halves = (own[d].astype(F32) + other[d].astype(F32)).astype(BF16)
        came.append(swap(halves, "expert", 2 * d))
    noted = (routes_f, gates_f, routes_b, gates_b)
    *noted, _ = lax.optimization_barrier((*noted, slot))
    home = kernel_call(
        functools.partial(home_kernel, topk, capacity),
        jax.ShapeDtypeStruct((groups, 2 * held, slot_rows), BF16),
        0,
        8 * groups * slot_rows * held,
    )(*noted)
    result_f, result_b = kernel_call(
        functools.partial(final_kernel, groups),
        (
            jax.ShapeDtypeStruct((held, width), BF16),
            jax.ShapeDtypeStruct((held, width), BF16),
        ),
        0,
        20 * held * width,
    )(moved_all[0], home, own, other, *came)
    return (result_f[None], result_b[None])


def solution(mesh):
    placed = (
        P("pipe", "expert", "dp"),
        P("pipe", "expert", "dp"),
        P("pipe", "expert", "dp"),
        P("pipe", "expert", None),
        P("pipe", "expert", None),
        P("pipe", "expert", None),
        P("pipe", "expert", None),
        P("pipe", "expert", "dp", None),
        P("pipe", "expert", "dp", None),
        P("pipe", "expert", None, "dp"),
    )
    return jax.shard_map(
        local,
        mesh=mesh,
        in_specs=placed,
        out_specs=(P("pipe", "expert", "dp"), P("pipe", "expert", "dp")),
        check_vma=False,
    )
```

```python
import functools

import jax
import jax.numpy as jnp
from jax import lax
from jax.experimental import pallas as pl
from jax.experimental.pallas import tpu as pltpu
from jax.sharding import PartitionSpec as P

BF16 = jnp.bfloat16
F32 = jnp.float32
LANES = 128
VMEM_LIMIT = 24 * 1024 * 1024


def in_vmem(x):
    return pltpu.with_memory_space_constraint(x, pltpu.VMEM)


def in_hbm(x):
    return pltpu.with_memory_space_constraint(x, pltpu.HBM)


def kernel_call(body, out_shape, flops, bytes_accessed):
    return pl.pallas_call(
        body,
        out_shape=out_shape,
        compiler_params=pltpu.CompilerParams(vmem_limit_bytes=VMEM_LIMIT),
        cost_estimate=pl.CostEstimate(flops=flops, bytes_accessed=bytes_accessed, transcendentals=0),
    )


def swap(x, axis, bit):
    peers = lax.axis_size(axis)
    return lax.ppermute(x, axis, [(i, i ^ bit) for i in range(peers)])


def mixed(x, even, odd):
    peers = lax.axis_size("expert")
    parts = lax.axis_size("dp")
    pairs = [
        (i * parts + k, i * parts + (k ^ (odd if i % 2 else even)))
        for i in range(peers)
        for k in range(parts)
    ]
    return lax.ppermute(x, ("expert", "dp"), pairs)


def onward(x, bit):
    sections = lax.axis_size("pipe")
    peers = lax.axis_size("expert")
    pairs = [
        (s * peers + i, (s + 1) % sections * peers + (i ^ bit))
        for s in range(sections)
        for i in range(peers)
    ]
    return lax.ppermute(x, ("pipe", "expert"), pairs)


def pack_kernel(x_hbm, c_hbm, b_hbm, *refs):
    rows, width = b_hbm.shape
    noted, (moved_ref, saved_ref, *held, sems) = refs[:4], refs[4:]
    pairs = list(zip(noted, held)) + [
        (x_hbm, moved_ref.at[pl.ds(0, rows)]),
        (c_hbm, moved_ref.at[pl.ds(rows, rows)]),
        (b_hbm, saved_ref.at[:, pl.ds(0, width)]),
    ]
    copies = [
        pltpu.make_async_copy(source, target, sems.at[i]) for i, (source, target) in enumerate(pairs)
    ]
    for copy in copies:
        copy.start()
    for copy in copies[:4]:
        copy.wait()
    notes = jnp.concatenate([r[...].astype(F32) for r in held], axis=0)
    for first in range(0, saved_ref.shape[1] - width, LANES):
        block = first // LANES * rows
        part = notes[block : block + rows]
        part = jnp.pad(part, ((0, rows - part.shape[0]), (0, LANES - part.shape[1])))
        saved_ref[:, width + first : width + first + LANES] = part.astype(BF16)
    for copy in copies[4:]:
        copy.wait()


def fetch_kernel(*refs):
    count = len(refs) // 2
    sems = refs[-1]
    copies = [
        pltpu.make_async_copy(refs[i], refs[count + i], sems.at[i]) for i in range(count)
    ]
    for copy in copies:
        copy.start()
    for copy in copies:
        copy.wait()


def unpack(saved, width, held, topk):
    per_tile = LANES // held
    tiles = []
    for first in range(0, len(saved), per_tile):
        tile = None
        for place, ref in enumerate(saved[first : first + per_tile]):
            spare = ref.shape[1] - width
            part = jnp.concatenate(
                [
                    ref[:, width + j * LANES : width + (j + 1) * LANES].astype(F32)
                    for j in range(spare // LANES)
                ],
                axis=0,
            )
            if place:
                part = pltpu.roll(part, place * held, 1)
            tile = part if tile is None else tile + part
        tiles.append(tile)
    notes = jnp.concatenate(tiles, axis=1) if len(tiles) > 1 else tiles[0]
    return notes[:, : len(saved) * held]


def places(notes, first, topk, expert, rows, base=0):
    tokens = notes.shape[1]
    hit = (notes[first : first + topk] == expert).astype(F32)
    named = jnp.sum(hit, axis=0, keepdims=True)
    weight = jnp.sum(hit * notes[first + topk : first + 2 * topk], axis=0, keepdims=True)
    earlier = lax.broadcasted_iota(jnp.int32, (tokens, tokens), 0) < lax.broadcasted_iota(
        jnp.int32, (tokens, tokens), 1
    )
    rank = jnp.dot(
        jnp.broadcast_to(named, (8, tokens)).astype(BF16),
        earlier.astype(BF16),
        preferred_element_type=F32,
    )[:1]
    row = lax.broadcasted_iota(jnp.int32, (rows, tokens), 0).astype(F32)
    place = jnp.where((row == rank + base) & (named > 0.0), 1.0, 0.0)
    return place, place * weight, named


def slots(named_f, named_b, held, capacity, slot_rows, rows):
    tokens = named_f.shape[1]
    total = tokens // held * slot_rows
    block = lax.broadcasted_iota(jnp.int32, (total, tokens), 0) // slot_rows
    before = lax.broadcasted_iota(jnp.int32, (total, tokens), 1) < block * held
    offset_f = jnp.sum(jnp.where(before, named_f, 0.0), axis=1, keepdims=True)
    offset_b = jnp.sum(jnp.where(before, named_b, 0.0), axis=1, keepdims=True)
    slot = lax.broadcasted_iota(jnp.int32, (total, 2 * rows), 0) % slot_rows
    row = lax.broadcasted_iota(jnp.int32, (total, 2 * rows), 1)
    slot_value, row_value = slot.astype(F32), row.astype(F32)
    taken_f = (slot < capacity) & (row < rows) & (row_value == offset_f + slot_value)
    taken_b = (
        (slot >= capacity)
        & (slot < 2 * capacity)
        & (row_value == offset_b + slot_value + float(rows - capacity))
    )
    return jnp.where(taken_f | taken_b, 1.0, 0.0)


def home_kernel(topk, capacity, rf_ref, gf_ref, rb_ref, gb_ref, home_ref):
    notes = jnp.concatenate(
        [r[...].astype(F32) for r in (rf_ref, gf_ref, rb_ref, gb_ref)], axis=0
    )
    groups, _, slot_rows = home_ref.shape
    mine = lax.axis_index("expert") // 2
    for d in range(groups):
        expert = (mine ^ d).astype(F32)
        _, weighed, _ = places(notes, 0, topk, expert, slot_rows)
        placed, _, _ = places(notes, 2 * topk, topk, expert, slot_rows, capacity)
        home_ref[d] = jnp.concatenate([weighed, placed], axis=1).T.astype(BF16)


def up_kernel(groups, topk, rows, capacity, slot_rows, *refs):
    moved = refs[: 2 * groups]
    saved = refs[2 * groups : 4 * groups]
    (
        w_g_ref,
        w_u_ref,
        w_d_ref,
        part_f_ref,
        part_b_ref,
        slot_ref,
    ) = refs[4 * groups :]
    held = moved[0].shape[0] // 2
    width = moved[0].shape[1]
    expert = (lax.axis_index("expert") // 2).astype(F32)
    notes = unpack(saved, width, held, topk)
    place_f, _, named_f = places(notes, 0, topk, expert, rows)
    place_b, weigh_b, named_b = places(notes, 2 * topk, topk, expert, rows)
    slot_ref[...] = slots(named_f, named_b, held, capacity, slot_rows, rows).astype(BF16)
    x_f = jnp.concatenate([r[:held, :] for r in moved], axis=0)
    c_b = jnp.concatenate([r[held:, :] for r in moved], axis=0)
    x_b = jnp.concatenate([r[:, :width] for r in saved], axis=0)
    rows_f = jnp.dot(place_f.astype(BF16), x_f, preferred_element_type=F32)
    rows_b = jnp.dot(place_b.astype(BF16), x_b, preferred_element_type=F32)
    grads_b = jnp.dot(weigh_b.astype(BF16), c_b, preferred_element_type=F32).astype(BF16)
    both = jnp.concatenate([rows_f, rows_b], axis=0).astype(BF16)
    gate = jnp.dot(both, w_g_ref[...], preferred_element_type=F32)
    upper = jnp.dot(both, w_u_ref[...], preferred_element_type=F32)
    dhid = lax.dot_general(grads_b, w_d_ref[...], (((1,), (1,)), ((), ())), preferred_element_type=F32)
    cut = part_f_ref.shape[1] - 2 * dhid.shape[1]
    part_f_ref[...] = jnp.concatenate([gate[:rows], upper[:rows], dhid[:, :cut]], axis=1).astype(BF16)
    part_b_ref[...] = jnp.concatenate([gate[rows:], upper[rows:], dhid[:, cut:]], axis=1).astype(BF16)


def out_kernel(a_ref, b_ref, w_d_ref, out_ref):
    units = w_d_ref.shape[0]
    gate = a_ref[:, :units].astype(F32) + b_ref[:, :units].astype(F32)
    upper = a_ref[:, units : 2 * units].astype(F32) + b_ref[:, units : 2 * units].astype(F32)
    hidden = (gate * jax.nn.sigmoid(gate) * upper).astype(BF16)
    out_ref[...] = jnp.dot(hidden, w_d_ref[...], preferred_element_type=F32)


def down_kernel(
    groups,
    rows,
    fa_ref,
    fb_ref,
    ba_ref,
    bb_ref,
    out_ref,
    slot_ref,
    w_g_ref,
    w_u_ref,
    own_ref,
    other_ref,
):
    units = w_g_ref.shape[1]
    total_b = ba_ref[...].astype(F32) + bb_ref[...].astype(F32)
    part_f = fa_ref[:, 2 * units :].astype(F32) + fb_ref[:, 2 * units :].astype(F32)
    gate_b, upper_b = total_b[:, :units], total_b[:, units : 2 * units]
    dhid = jnp.concatenate([part_f, total_b[:, 2 * units :]], axis=1)
    sigma = jax.nn.sigmoid(gate_b)
    slope = sigma * (1.0 + gate_b * (1.0 - sigma))
    dgate = (dhid * upper_b * slope).astype(BF16)
    dupper = (dhid * (gate_b * sigma)).astype(BF16)
    turned = (((1,), (1,)), ((), ()))
    grad = lax.dot_general(dgate, w_g_ref[...], turned, preferred_element_type=F32)
    grad = grad + lax.dot_general(dupper, w_u_ref[...], turned, preferred_element_type=F32)
    both = jnp.concatenate([out_ref[...], grad], axis=0).astype(BF16)
    full = jnp.dot(slot_ref[...], both, preferred_element_type=F32)
    slot_rows = own_ref.shape[1]
    for d in range(groups):
        for ref, block in ((own_ref, d), (other_ref, groups + d)):
            ref[d] = full[block * slot_rows : (block + 1) * slot_rows].astype(BF16)


def final_kernel(groups, moved_ref, home_ref, own_ref, other_ref, *refs):
    came = refs[: groups - 1]
    out_f_ref, out_b_ref = refs[groups - 1 :]
    held = out_f_ref.shape[0]
    result = moved_ref[...].astype(F32)
    for d in range(groups):
        for part in (own_ref[0], other_ref[0]) if d == 0 else (came[d - 1][...],):
            result = result + jnp.dot(home_ref[d], part, preferred_element_type=F32)
    out_f_ref[...] = result[:held].astype(BF16)
    out_b_ref[...] = result[held:].astype(BF16)


def local(
    carry_forward,
    carry_cotangent,
    saved_input,
    routes_forward,
    gates_forward,
    routes_backward,
    gates_backward,
    w_gate,
    w_up,
    w_down,
):
    peers = lax.axis_size("expert")
    experts = peers // 2
    groups = peers // 2
    held, width = carry_forward.shape[1:]
    hidden = w_gate.shape[3]
    topk = routes_forward.shape[2]
    capacity = min(held, max(6, held * topk // experts + 2))
    rows = -(-peers * capacity // 8) * 8
    cut = hidden * 2 // 4
    slot_rows = -(-2 * capacity // 8) * 8
    weight_bytes = 6 * width * hidden
    w_g, w_u, w_d = pl.pallas_call(
        fetch_kernel,
        out_shape=[pltpu.VMEM(w.shape[2:], BF16) for w in (w_gate, w_up, w_down)],
        in_specs=[pl.BlockSpec(memory_space=pltpu.HBM)] * 3,
        out_specs=[pl.BlockSpec(memory_space=pltpu.VMEM)] * 3,
        scratch_shapes=[pltpu.SemaphoreType.DMA((3,))],
        compiler_params=pltpu.CompilerParams(vmem_limit_bytes=VMEM_LIMIT),
        cost_estimate=pl.CostEstimate(flops=0, bytes_accessed=2 * weight_bytes, transcendentals=0),
    )(*[in_hbm(w[0, 0]) for w in (w_gate, w_up, w_down)])
    routes_f, gates_f, routes_b, gates_b = [
        jnp.swapaxes(a[0], 0, 1)
        for a in (routes_forward, gates_forward, routes_backward, gates_backward)
    ]
    spare = -(-4 * topk // held) * LANES
    moved, saved = pl.pallas_call(
        pack_kernel,
        out_shape=[
            jax.ShapeDtypeStruct((2 * held, width), BF16),
            jax.ShapeDtypeStruct((held, width + spare), BF16),
        ],
        in_specs=[pl.BlockSpec(memory_space=pltpu.HBM)] * 7,
        out_specs=[pl.BlockSpec(memory_space=pltpu.VMEM)] * 2,
        scratch_shapes=[pltpu.VMEM(a.shape, a.dtype) for a in (routes_f, gates_f, routes_b, gates_b)]
        + [pltpu.SemaphoreType.DMA((7,))],
        compiler_params=pltpu.CompilerParams(vmem_limit_bytes=VMEM_LIMIT),
        cost_estimate=pl.CostEstimate(flops=0, bytes_accessed=12 * held * width, transcendentals=0),
    )(
        *[in_hbm(a[0]) for a in (carry_forward, carry_cotangent, saved_input)],
        *[in_hbm(a) for a in (routes_f, gates_f, routes_b, gates_b)],
    )
    moved_all = [onward(moved, 2 * d) for d in range(groups)]
    moved_all = [onward(moved, 2 * d) for d in range(groups)]
    saved_all = [saved] + [swap(saved, "expert", 2 * d) for d in range(1, groups)]
    saved_all = saved_all + [swap(x, "expert", 1) for x in saved_all]
    moved_all[0], w_g, w_u, w_d = lax.optimization_barrier((moved_all[0], w_g, w_u, w_d))
    moved_all[1], w_g = lax.optimization_barrier((moved_all[1], w_g))
    w_g, w_u, w_d = in_vmem(w_g), in_vmem(w_u), in_vmem(w_d)
    moved_swap = []
    for x in moved_all:
        if moved_swap:
            x, *_ = lax.optimization_barrier((x, moved_swap[-1], *saved_all))
        moved_swap.append(swap(x, "expert", 1))
    moved_all = moved_all + moved_swap
    part_f, part_b, slot = kernel_call(
        functools.partial(up_kernel, groups, topk, rows, capacity, slot_rows),
        (
            jax.ShapeDtypeStruct((rows, 2 * hidden + cut), BF16),
            jax.ShapeDtypeStruct((rows, 3 * hidden - cut), BF16),
            jax.ShapeDtypeStruct((peers * slot_rows, 2 * rows), BF16),
        ),
        10 * rows * width * hidden,
        weight_bytes,
    )(*moved_all, *saved_all, w_g, w_u, w_d)
    bits = [1 << i for i in range(lax.axis_size("dp").bit_length() - 1)]
    last = bits[-1]
    for up, down in zip(bits, bits[::-1]):
        came_f = mixed(part_f, up, down)
        came_b = mixed(part_b, up, down)
        if up == last:
            break
        part_f = (part_f.astype(F32) + came_f.astype(F32)).astype(BF16)
        part_b = (part_b.astype(F32) + came_b.astype(F32)).astype(BF16)
    out_f = kernel_call(
        out_kernel,
        jax.ShapeDtypeStruct((rows, width), F32),
        2 * rows * width * hidden,
        2 * width * hidden,
    )(part_f, came_f, w_d)
    own, other = kernel_call(
        functools.partial(down_kernel, groups, rows),
        [jax.ShapeDtypeStruct((groups, slot_rows, width), BF16)] * 2,
        4 * rows * width * hidden,
        4 * width * hidden,
    )(part_f, came_f, part_b, came_b, out_f, slot, w_g, w_u)
    other = swap(other, "expert", 1)
    came = []
    for d in range(1, groups):
        halves = (own[d].astype(F32) + other[d].astype(F32)).astype(BF16)
        came.append(swap(halves, "expert", 2 * d))
    noted = (routes_f, gates_f, routes_b, gates_b)
    *noted, _ = lax.optimization_barrier((*noted, slot))
    home = kernel_call(
        functools.partial(home_kernel, topk, capacity),
        jax.ShapeDtypeStruct((groups, 2 * held, slot_rows), BF16),
        0,
        8 * groups * slot_rows * held,
    )(*noted)
    result_f, result_b = kernel_call(
        functools.partial(final_kernel, groups),
        (
            jax.ShapeDtypeStruct((held, width), BF16),
            jax.ShapeDtypeStruct((held, width), BF16),
        ),
        0,
        20 * held * width,
    )(moved_all[0], home, own, other, *came)
    return (result_f[None], result_b[None])


def solution(mesh):
    placed = (
        P("pipe", "expert", "dp"),
        P("pipe", "expert", "dp"),
        P("pipe", "expert", "dp"),
        P("pipe", "expert", None),
        P("pipe", "expert", None),
        P("pipe", "expert", None),
        P("pipe", "expert", None),
        P("pipe", "expert", "dp", None),
        P("pipe", "expert", "dp", None),
        P("pipe", "expert", None, "dp"),
    )
    return jax.shard_map(
        local,
        mesh=mesh,
        in_specs=placed,
        out_specs=(P("pipe", "expert", "dp"), P("pipe", "expert", "dp")),
        check_vma=False,
    )
```

```python
import functools

import jax
import jax.numpy as jnp
from jax import lax
from jax.experimental import pallas as pl
from jax.experimental.pallas import tpu as pltpu
from jax.sharding import PartitionSpec as P

BF16 = jnp.bfloat16
F32 = jnp.float32
LANES = 128
VMEM_LIMIT = 24 * 1024 * 1024


def in_vmem(x):
    return pltpu.with_memory_space_constraint(x, pltpu.VMEM)


def in_hbm(x):
    return pltpu.with_memory_space_constraint(x, pltpu.HBM)


def kernel_call(body, out_shape, flops, bytes_accessed):
    return pl.pallas_call(
        body,
        out_shape=out_shape,
        compiler_params=pltpu.CompilerParams(vmem_limit_bytes=VMEM_LIMIT),
        cost_estimate=pl.CostEstimate(flops=flops, bytes_accessed=bytes_accessed, transcendentals=0),
    )


def swap(x, axis, bit):
    peers = lax.axis_size(axis)
    return lax.ppermute(x, axis, [(i, i ^ bit) for i in range(peers)])


def mixed(x, even, odd):
    peers = lax.axis_size("expert")
    parts = lax.axis_size("dp")
    pairs = [
        (i * parts + k, i * parts + (k ^ (odd if i % 2 else even)))
        for i in range(peers)
        for k in range(parts)
    ]
    return lax.ppermute(x, ("expert", "dp"), pairs)


def onward(x, bit):
    sections = lax.axis_size("pipe")
    peers = lax.axis_size("expert")
    pairs = [
        (s * peers + i, (s + 1) % sections * peers + (i ^ bit))
        for s in range(sections)
        for i in range(peers)
    ]
    return lax.ppermute(x, ("pipe", "expert"), pairs)


def pack_kernel(x_hbm, c_hbm, b_hbm, *refs):
    rows, width = b_hbm.shape
    noted, (moved_ref, saved_ref, *held, sems) = refs[:4], refs[4:]
    pairs = list(zip(noted, held)) + [
        (x_hbm, moved_ref.at[pl.ds(0, rows)]),
        (c_hbm, moved_ref.at[pl.ds(rows, rows)]),
        (b_hbm, saved_ref.at[:, pl.ds(0, width)]),
    ]
    copies = [
        pltpu.make_async_copy(source, target, sems.at[i]) for i, (source, target) in enumerate(pairs)
    ]
    for copy in copies:
        copy.start()
    for copy in copies[:4]:
        copy.wait()
    notes = jnp.concatenate([r[...].astype(F32) for r in held], axis=0)
    for first in range(0, saved_ref.shape[1] - width, LANES):
        block = first // LANES * rows
        part = notes[block : block + rows]
        part = jnp.pad(part, ((0, rows - part.shape[0]), (0, LANES - part.shape[1])))
        saved_ref[:, width + first : width + first + LANES] = part.astype(BF16)
    for copy in copies[4:]:
        copy.wait()


def fetch_kernel(*refs):
    count = len(refs) // 2
    sems = refs[-1]
    copies = [
        pltpu.make_async_copy(refs[i], refs[count + i], sems.at[i]) for i in range(count)
    ]
    for copy in copies:
        copy.start()
    for copy in copies:
        copy.wait()


def unpack(saved, width, held, topk):
    per_tile = LANES // held
    tiles = []
    for first in range(0, len(saved), per_tile):
        tile = None
        for place, ref in enumerate(saved[first : first + per_tile]):
            spare = ref.shape[1] - width
            part = jnp.concatenate(
                [
                    ref[:, width + j * LANES : width + (j + 1) * LANES].astype(F32)
                    for j in range(spare // LANES)
                ],
                axis=0,
            )
            if place:
                part = pltpu.roll(part, place * held, 1)
            tile = part if tile is None else tile + part
        tiles.append(tile)
    notes = jnp.concatenate(tiles, axis=1) if len(tiles) > 1 else tiles[0]
    return notes[:, : len(saved) * held]


def places(notes, first, topk, expert, rows, base=0):
    tokens = notes.shape[1]
    hit = (notes[first : first + topk] == expert).astype(F32)
    named = jnp.sum(hit, axis=0, keepdims=True)
    weight = jnp.sum(hit * notes[first + topk : first + 2 * topk], axis=0, keepdims=True)
    earlier = lax.broadcasted_iota(jnp.int32, (tokens, tokens), 0) < lax.broadcasted_iota(
        jnp.int32, (tokens, tokens), 1
    )
    rank = jnp.dot(
        jnp.broadcast_to(named, (8, tokens)).astype(BF16),
        earlier.astype(BF16),
        preferred_element_type=F32,
    )[:1]
    row = lax.broadcasted_iota(jnp.int32, (rows, tokens), 0).astype(F32)
    place = jnp.where((row == rank + base) & (named > 0.0), 1.0, 0.0)
    return place, place * weight, named


def slots(named_f, named_b, held, capacity, slot_rows, rows):
    tokens = named_f.shape[1]
    total = tokens // held * slot_rows
    block = lax.broadcasted_iota(jnp.int32, (total, tokens), 0) // slot_rows
    before = lax.broadcasted_iota(jnp.int32, (total, tokens), 1) < block * held
    offset_f = jnp.sum(jnp.where(before, named_f, 0.0), axis=1, keepdims=True)
    offset_b = jnp.sum(jnp.where(before, named_b, 0.0), axis=1, keepdims=True)
    slot = lax.broadcasted_iota(jnp.int32, (total, 2 * rows), 0) % slot_rows
    row = lax.broadcasted_iota(jnp.int32, (total, 2 * rows), 1)
    slot_value, row_value = slot.astype(F32), row.astype(F32)
    taken_f = (slot < capacity) & (row < rows) & (row_value == offset_f + slot_value)
    taken_b = (
        (slot >= capacity)
        & (slot < 2 * capacity)
        & (row_value == offset_b + slot_value + float(rows - capacity))
    )
    return jnp.where(taken_f | taken_b, 1.0, 0.0)


def home_kernel(topk, capacity, rf_ref, gf_ref, rb_ref, gb_ref, home_ref):
    notes = jnp.concatenate(
        [r[...].astype(F32) for r in (rf_ref, gf_ref, rb_ref, gb_ref)], axis=0
    )
    groups, _, slot_rows = home_ref.shape
    mine = lax.axis_index("expert") // 2
    for d in range(groups):
        expert = (mine ^ d).astype(F32)
        _, weighed, _ = places(notes, 0, topk, expert, slot_rows)
        placed, _, _ = places(notes, 2 * topk, topk, expert, slot_rows, capacity)
        home_ref[d] = jnp.concatenate([weighed, placed], axis=1).T.astype(BF16)


def up_kernel(groups, topk, rows, capacity, slot_rows, *refs):
    moved = refs[: 2 * groups]
    saved = refs[2 * groups : 4 * groups]
    (
        w_g_ref,
        w_u_ref,
        w_d_ref,
        part_f_ref,
        part_b_ref,
        slot_ref,
    ) = refs[4 * groups :]
    held = moved[0].shape[0] // 2
    width = moved[0].shape[1]
    expert = (lax.axis_index("expert") // 2).astype(F32)
    notes = unpack(saved, width, held, topk)
    place_f, _, named_f = places(notes, 0, topk, expert, rows)
    place_b, weigh_b, named_b = places(notes, 2 * topk, topk, expert, rows)
    slot_ref[...] = slots(named_f, named_b, held, capacity, slot_rows, rows).astype(BF16)
    x_f = jnp.concatenate([r[:held, :] for r in moved], axis=0)
    c_b = jnp.concatenate([r[held:, :] for r in moved], axis=0)
    x_b = jnp.concatenate([r[:, :width] for r in saved], axis=0)
    rows_f = jnp.dot(place_f.astype(BF16), x_f, preferred_element_type=F32)
    rows_b = jnp.dot(place_b.astype(BF16), x_b, preferred_element_type=F32)
    grads_b = jnp.dot(weigh_b.astype(BF16), c_b, preferred_element_type=F32).astype(BF16)
    both = jnp.concatenate([rows_f, rows_b], axis=0).astype(BF16)
    gate = jnp.dot(both, w_g_ref[...], preferred_element_type=F32)
    upper = jnp.dot(both, w_u_ref[...], preferred_element_type=F32)
    dhid = lax.dot_general(grads_b, w_d_ref[...], (((1,), (1,)), ((), ())), preferred_element_type=F32)
    part_f_ref[...] = jnp.concatenate([gate[:rows], upper[:rows]], axis=1).astype(BF16)
    part_b_ref[...] = jnp.concatenate([gate[rows:], upper[rows:], dhid], axis=1).astype(BF16)


def grad_kernel(a_ref, b_ref, w_g_ref, w_u_ref, grad_ref):
    units = w_g_ref.shape[1]
    total = a_ref[...].astype(F32) + b_ref[...].astype(F32)
    gate, upper, dhid = [total[:, i * units : (i + 1) * units] for i in range(3)]
    sigma = jax.nn.sigmoid(gate)
    slope = sigma * (1.0 + gate * (1.0 - sigma))
    dgate = (dhid * upper * slope).astype(BF16)
    dupper = (dhid * (gate * sigma)).astype(BF16)
    turned = (((1,), (1,)), ((), ()))
    grad = lax.dot_general(dgate, w_g_ref[...], turned, preferred_element_type=F32)
    grad = grad + lax.dot_general(dupper, w_u_ref[...], turned, preferred_element_type=F32)
    grad_ref[...] = grad


def down_kernel(groups, a_ref, b_ref, grad_ref, slot_ref, w_d_ref, own_ref, other_ref):
    units = w_d_ref.shape[0]
    total = a_ref[...].astype(F32) + b_ref[...].astype(F32)
    gate, upper = total[:, :units], total[:, units:]
    hidden = (gate * jax.nn.sigmoid(gate) * upper).astype(BF16)
    out = jnp.dot(hidden, w_d_ref[...], preferred_element_type=F32)
    both = jnp.concatenate([out, grad_ref[...]], axis=0).astype(BF16)
    full = jnp.dot(slot_ref[...], both, preferred_element_type=F32)
    slot_rows = own_ref.shape[1]
    for d in range(groups):
        for ref, block in ((own_ref, d), (other_ref, groups + d)):
            ref[d] = full[block * slot_rows : (block + 1) * slot_rows].astype(BF16)


def final_kernel(groups, moved_ref, home_ref, own_ref, other_ref, *refs):
    came = refs[: groups - 1]
    out_f_ref, out_b_ref = refs[groups - 1 :]
    held = out_f_ref.shape[0]
    result = moved_ref[...].astype(F32)
    for d in range(groups):
        for part in (own_ref[0], other_ref[0]) if d == 0 else (came[d - 1][...],):
            result = result + jnp.dot(home_ref[d], part, preferred_element_type=F32)
    out_f_ref[...] = result[:held].astype(BF16)
    out_b_ref[...] = result[held:].astype(BF16)


def local(
    carry_forward,
    carry_cotangent,
    saved_input,
    routes_forward,
    gates_forward,
    routes_backward,
    gates_backward,
    w_gate,
    w_up,
    w_down,
):
    peers = lax.axis_size("expert")
    experts = peers // 2
    groups = peers // 2
    held, width = carry_forward.shape[1:]
    hidden = w_gate.shape[3]
    topk = routes_forward.shape[2]
    capacity = min(held, max(6, held * topk // experts + 2))
    rows = -(-peers * capacity // 8) * 8
    slot_rows = -(-2 * capacity // 8) * 8
    weight_bytes = 6 * width * hidden
    w_g, w_u, w_d = pl.pallas_call(
        fetch_kernel,
        out_shape=[pltpu.VMEM(w.shape[2:], BF16) for w in (w_gate, w_up, w_down)],
        in_specs=[pl.BlockSpec(memory_space=pltpu.HBM)] * 3,
        out_specs=[pl.BlockSpec(memory_space=pltpu.VMEM)] * 3,
        scratch_shapes=[pltpu.SemaphoreType.DMA((3,))],
        compiler_params=pltpu.CompilerParams(vmem_limit_bytes=VMEM_LIMIT),
        cost_estimate=pl.CostEstimate(flops=0, bytes_accessed=2 * weight_bytes, transcendentals=0),
    )(*[in_hbm(w[0, 0]) for w in (w_gate, w_up, w_down)])
    routes_f, gates_f, routes_b, gates_b = [
        jnp.swapaxes(a[0], 0, 1)
        for a in (routes_forward, gates_forward, routes_backward, gates_backward)
    ]
    spare = -(-4 * topk // held) * LANES
    moved, saved = pl.pallas_call(
        pack_kernel,
        out_shape=[
            jax.ShapeDtypeStruct((2 * held, width), BF16),
            jax.ShapeDtypeStruct((held, width + spare), BF16),
        ],
        in_specs=[pl.BlockSpec(memory_space=pltpu.HBM)] * 7,
        out_specs=[pl.BlockSpec(memory_space=pltpu.VMEM)] * 2,
        scratch_shapes=[pltpu.VMEM(a.shape, a.dtype) for a in (routes_f, gates_f, routes_b, gates_b)]
        + [pltpu.SemaphoreType.DMA((7,))],
        compiler_params=pltpu.CompilerParams(vmem_limit_bytes=VMEM_LIMIT),
        cost_estimate=pl.CostEstimate(flops=0, bytes_accessed=12 * held * width, transcendentals=0),
    )(
        *[in_hbm(a[0]) for a in (carry_forward, carry_cotangent, saved_input)],
        *[in_hbm(a) for a in (routes_f, gates_f, routes_b, gates_b)],
    )
    moved_all = [onward(moved, 2 * d) for d in range(groups)]
    moved_all = [onward(moved, 2 * d) for d in range(groups)]
    saved_all = [saved] + [swap(saved, "expert", 2 * d) for d in range(1, groups)]
    saved_all = saved_all + [swap(x, "expert", 1) for x in saved_all]
    moved_all[0], w_g, w_u, w_d = lax.optimization_barrier((moved_all[0], w_g, w_u, w_d))
    moved_all[1], w_g = lax.optimization_barrier((moved_all[1], w_g))
    w_g, w_u, w_d = in_vmem(w_g), in_vmem(w_u), in_vmem(w_d)
    moved_swap = []
    for x in moved_all:
        if moved_swap:
            x, *_ = lax.optimization_barrier((x, moved_swap[-1], *saved_all))
        moved_swap.append(swap(x, "expert", 1))
    moved_all = moved_all + moved_swap
    part_f, part_b, slot = kernel_call(
        functools.partial(up_kernel, groups, topk, rows, capacity, slot_rows),
        (
            jax.ShapeDtypeStruct((rows, 2 * hidden), BF16),
            jax.ShapeDtypeStruct((rows, 3 * hidden), BF16),
            jax.ShapeDtypeStruct((peers * slot_rows, 2 * rows), BF16),
        ),
        10 * rows * width * hidden,
        weight_bytes,
    )(*moved_all, *saved_all, w_g, w_u, w_d)
    bits = [1 << i for i in range(lax.axis_size("dp").bit_length() - 1)]
    last = bits[-1]
    for up, down in zip(bits, bits[::-1]):
        came_f = mixed(part_f, up, down)
        came_b = mixed(part_b, up, down)
        if up == last:
            break
        part_f = (part_f.astype(F32) + came_f.astype(F32)).astype(BF16)
        part_b = (part_b.astype(F32) + came_b.astype(F32)).astype(BF16)
    grad = kernel_call(
        grad_kernel,
        jax.ShapeDtypeStruct((rows, width), F32),
        4 * rows * width * hidden,
        4 * width * hidden,
    )(part_b, came_b, w_g, w_u)
    own, other = kernel_call(
        functools.partial(down_kernel, groups),
        [jax.ShapeDtypeStruct((groups, slot_rows, width), BF16)] * 2,
        2 * rows * width * hidden,
        2 * width * hidden,
    )(part_f, came_f, grad, slot, w_d)
    other = swap(other, "expert", 1)
    came = []
    for d in range(1, groups):
        halves = (own[d].astype(F32) + other[d].astype(F32)).astype(BF16)
        came.append(swap(halves, "expert", 2 * d))
    noted = (routes_f, gates_f, routes_b, gates_b)
    *noted, _ = lax.optimization_barrier((*noted, slot))
    home = kernel_call(
        functools.partial(home_kernel, topk, capacity),
        jax.ShapeDtypeStruct((groups, 2 * held, slot_rows), BF16),
        0,
        8 * groups * slot_rows * held,
    )(*noted)
    result_f, result_b = kernel_call(
        functools.partial(final_kernel, groups),
        (
            jax.ShapeDtypeStruct((held, width), BF16),
            jax.ShapeDtypeStruct((held, width), BF16),
        ),
        0,
        20 * held * width,
    )(moved_all[0], home, own, other, *came)
    return (result_f[None], result_b[None])


def solution(mesh):
    placed = (
        P("pipe", "expert", "dp"),
        P("pipe", "expert", "dp"),
        P("pipe", "expert", "dp"),
        P("pipe", "expert", None),
        P("pipe", "expert", None),
        P("pipe", "expert", None),
        P("pipe", "expert", None),
        P("pipe", "expert", "dp", None),
        P("pipe", "expert", "dp", None),
        P("pipe", "expert", None, "dp"),
    )
    return jax.shard_map(
        local,
        mesh=mesh,
        in_specs=placed,
        out_specs=(P("pipe", "expert", "dp"), P("pipe", "expert", "dp")),
        check_vma=False,
    )
```

```python
import functools

import jax
import jax.numpy as jnp
from jax import lax
from jax.experimental import pallas as pl
from jax.experimental.pallas import tpu as pltpu
from jax.sharding import PartitionSpec as P

BF16 = jnp.bfloat16
F32 = jnp.float32
LANES = 128
VMEM_LIMIT = 24 * 1024 * 1024


def in_vmem(x):
    return pltpu.with_memory_space_constraint(x, pltpu.VMEM)


def in_hbm(x):
    return pltpu.with_memory_space_constraint(x, pltpu.HBM)


def kernel_call(body, out_shape, flops, bytes_accessed):
    return pl.pallas_call(
        body,
        out_shape=out_shape,
        compiler_params=pltpu.CompilerParams(vmem_limit_bytes=VMEM_LIMIT),
        cost_estimate=pl.CostEstimate(flops=flops, bytes_accessed=bytes_accessed, transcendentals=0),
    )


def swap(x, axis, bit):
    peers = lax.axis_size(axis)
    return lax.ppermute(x, axis, [(i, i ^ bit) for i in range(peers)])


def mixed(x, even, odd):
    peers = lax.axis_size("expert")
    parts = lax.axis_size("dp")
    pairs = [
        (i * parts + k, i * parts + (k ^ (odd if i % 2 else even)))
        for i in range(peers)
        for k in range(parts)
    ]
    return lax.ppermute(x, ("expert", "dp"), pairs)


def onward(x, bit):
    sections = lax.axis_size("pipe")
    peers = lax.axis_size("expert")
    pairs = [
        (s * peers + i, (s + 1) % sections * peers + (i ^ bit))
        for s in range(sections)
        for i in range(peers)
    ]
    return lax.ppermute(x, ("pipe", "expert"), pairs)


def pack_kernel(x_hbm, c_hbm, b_hbm, *refs):
    rows, width = b_hbm.shape
    noted, (moved_ref, saved_ref, *held, sems) = refs[:4], refs[4:]
    pairs = list(zip(noted, held)) + [
        (x_hbm, moved_ref.at[pl.ds(0, rows)]),
        (c_hbm, moved_ref.at[pl.ds(rows, rows)]),
        (b_hbm, saved_ref.at[:, pl.ds(0, width)]),
    ]
    copies = [
        pltpu.make_async_copy(source, target, sems.at[i]) for i, (source, target) in enumerate(pairs)
    ]
    for copy in copies:
        copy.start()
    for copy in copies[:4]:
        copy.wait()
    notes = jnp.concatenate([r[...].astype(F32) for r in held], axis=0)
    for first in range(0, saved_ref.shape[1] - width, LANES):
        block = first // LANES * rows
        part = notes[block : block + rows]
        part = jnp.pad(part, ((0, rows - part.shape[0]), (0, LANES - part.shape[1])))
        saved_ref[:, width + first : width + first + LANES] = part.astype(BF16)
    for copy in copies[4:]:
        copy.wait()


def fetch_kernel(*refs):
    count = len(refs) // 2
    sems = refs[-1]
    copies = [
        pltpu.make_async_copy(refs[i], refs[count + i], sems.at[i]) for i in range(count)
    ]
    for copy in copies:
        copy.start()
    for copy in copies:
        copy.wait()


def unpack(saved, width, held, topk):
    per_tile = LANES // held
    tiles = []
    for first in range(0, len(saved), per_tile):
        tile = None
        for place, ref in enumerate(saved[first : first + per_tile]):
            spare = ref.shape[1] - width
            part = jnp.concatenate(
                [
                    ref[:, width + j * LANES : width + (j + 1) * LANES].astype(F32)
                    for j in range(spare // LANES)
                ],
                axis=0,
            )
            if place:
                part = pltpu.roll(part, place * held, 1)
            tile = part if tile is None else tile + part
        tiles.append(tile)
    notes = jnp.concatenate(tiles, axis=1) if len(tiles) > 1 else tiles[0]
    return notes[:, : len(saved) * held]


def places(notes, first, topk, expert, rows, base=0):
    tokens = notes.shape[1]
    hit = (notes[first : first + topk] == expert).astype(F32)
    named = jnp.sum(hit, axis=0, keepdims=True)
    weight = jnp.sum(hit * notes[first + topk : first + 2 * topk], axis=0, keepdims=True)
    earlier = lax.broadcasted_iota(jnp.int32, (tokens, tokens), 0) < lax.broadcasted_iota(
        jnp.int32, (tokens, tokens), 1
    )
    rank = jnp.dot(
        jnp.broadcast_to(named, (8, tokens)).astype(BF16),
        earlier.astype(BF16),
        preferred_element_type=F32,
    )[:1]
    row = lax.broadcasted_iota(jnp.int32, (rows, tokens), 0).astype(F32)
    place = jnp.where((row == rank + base) & (named > 0.0), 1.0, 0.0)
    return place, place * weight, named


def slots(named_f, named_b, held, capacity, slot_rows, rows):
    tokens = named_f.shape[1]
    total = tokens // held * slot_rows
    block = lax.broadcasted_iota(jnp.int32, (total, tokens), 0) // slot_rows
    before = lax.broadcasted_iota(jnp.int32, (total, tokens), 1) < block * held
    offset_f = jnp.sum(jnp.where(before, named_f, 0.0), axis=1, keepdims=True)
    offset_b = jnp.sum(jnp.where(before, named_b, 0.0), axis=1, keepdims=True)
    slot = lax.broadcasted_iota(jnp.int32, (total, 2 * rows), 0) % slot_rows
    row = lax.broadcasted_iota(jnp.int32, (total, 2 * rows), 1)
    slot_value, row_value = slot.astype(F32), row.astype(F32)
    taken_f = (slot < capacity) & (row < rows) & (row_value == offset_f + slot_value)
    taken_b = (
        (slot >= capacity)
        & (slot < 2 * capacity)
        & (row_value == offset_b + slot_value + float(rows - capacity))
    )
    return jnp.where(taken_f | taken_b, 1.0, 0.0)


def home_kernel(topk, capacity, rf_ref, gf_ref, rb_ref, gb_ref, home_ref):
    notes = jnp.concatenate(
        [r[...].astype(F32) for r in (rf_ref, gf_ref, rb_ref, gb_ref)], axis=0
    )
    groups, _, slot_rows = home_ref.shape
    mine = lax.axis_index("expert") // 2
    for d in range(groups):
        expert = (mine ^ d).astype(F32)
        _, weighed, _ = places(notes, 0, topk, expert, slot_rows)
        placed, _, _ = places(notes, 2 * topk, topk, expert, slot_rows, capacity)
        home_ref[d] = jnp.concatenate([weighed, placed], axis=1).T.astype(BF16)


def up_kernel(groups, topk, rows, capacity, slot_rows, *refs):
    moved = refs[: 2 * groups]
    saved = refs[2 * groups : 4 * groups]
    (
        w_g_ref,
        w_u_ref,
        w_d_ref,
        part_f_ref,
        part_b_ref,
        slot_ref,
    ) = refs[4 * groups :]
    held = moved[0].shape[0] // 2
    width = moved[0].shape[1]
    expert = (lax.axis_index("expert") // 2).astype(F32)
    notes = unpack(saved, width, held, topk)
    place_f, _, named_f = places(notes, 0, topk, expert, rows)
    place_b, weigh_b, named_b = places(notes, 2 * topk, topk, expert, rows)
    slot_ref[...] = slots(named_f, named_b, held, capacity, slot_rows, rows).astype(BF16)
    x_f = jnp.concatenate([r[:held, :] for r in moved], axis=0)
    c_b = jnp.concatenate([r[held:, :] for r in moved], axis=0)
    x_b = jnp.concatenate([r[:, :width] for r in saved], axis=0)
    rows_f = jnp.dot(place_f.astype(BF16), x_f, preferred_element_type=F32)
    rows_b = jnp.dot(place_b.astype(BF16), x_b, preferred_element_type=F32)
    grads_b = jnp.dot(weigh_b.astype(BF16), c_b, preferred_element_type=F32).astype(BF16)
    both = jnp.concatenate([rows_f, rows_b], axis=0).astype(BF16)
    gate = jnp.dot(both, w_g_ref[...], preferred_element_type=F32)
    upper = jnp.dot(both, w_u_ref[...], preferred_element_type=F32)
    dhid = lax.dot_general(grads_b, w_d_ref[...], (((1,), (1,)), ((), ())), preferred_element_type=F32)
    part_f_ref[...] = jnp.concatenate([gate[:rows], upper[:rows]], axis=1).astype(BF16)
    part_b_ref[...] = jnp.concatenate([gate[rows:], upper[rows:], dhid], axis=1).astype(BF16)


def grad_kernel(a_ref, b_ref, w_g_ref, w_u_ref, grad_ref):
    units = w_g_ref.shape[1]
    total = a_ref[...].astype(F32) + b_ref[...].astype(F32)
    gate, upper, dhid = [total[:, i * units : (i + 1) * units] for i in range(3)]
    sigma = jax.nn.sigmoid(gate)
    slope = sigma * (1.0 + gate * (1.0 - sigma))
    dgate = (dhid * upper * slope).astype(BF16)
    dupper = (dhid * (gate * sigma)).astype(BF16)
    turned = (((1,), (1,)), ((), ()))
    grad = lax.dot_general(dgate, w_g_ref[...], turned, preferred_element_type=F32)
    grad = grad + lax.dot_general(dupper, w_u_ref[...], turned, preferred_element_type=F32)
    grad_ref[...] = grad.astype(BF16)


def down_kernel(groups, a_ref, b_ref, grad_ref, slot_ref, w_d_ref, own_ref, other_ref):
    units = w_d_ref.shape[0]
    total = a_ref[...].astype(F32) + b_ref[...].astype(F32)
    gate, upper = total[:, :units], total[:, units:]
    hidden = (gate * jax.nn.sigmoid(gate) * upper).astype(BF16)
    out = jnp.dot(hidden, w_d_ref[...], preferred_element_type=F32)
    both = jnp.concatenate([out, grad_ref[...].astype(F32)], axis=0).astype(BF16)
    full = jnp.dot(slot_ref[...], both, preferred_element_type=F32)
    slot_rows = own_ref.shape[1]
    for d in range(groups):
        for ref, block in ((own_ref, d), (other_ref, groups + d)):
            ref[d] = full[block * slot_rows : (block + 1) * slot_rows].astype(BF16)


def final_kernel(groups, moved_ref, home_ref, own_ref, other_ref, *refs):
    came = refs[: groups - 1]
    out_f_ref, out_b_ref = refs[groups - 1 :]
    held = out_f_ref.shape[0]
    result = moved_ref[...].astype(F32)
    for d in range(groups):
        for part in (own_ref[0], other_ref[0]) if d == 0 else (came[d - 1][...],):
            result = result + jnp.dot(home_ref[d], part, preferred_element_type=F32)
    out_f_ref[...] = result[:held].astype(BF16)
    out_b_ref[...] = result[held:].astype(BF16)


def local(
    carry_forward,
    carry_cotangent,
    saved_input,
    routes_forward,
    gates_forward,
    routes_backward,
    gates_backward,
    w_gate,
    w_up,
    w_down,
):
    peers = lax.axis_size("expert")
    experts = peers // 2
    groups = peers // 2
    held, width = carry_forward.shape[1:]
    hidden = w_gate.shape[3]
    topk = routes_forward.shape[2]
    capacity = min(held, max(6, held * topk // experts + 2))
    rows = -(-peers * capacity // 8) * 8
    slot_rows = -(-2 * capacity // 8) * 8
    weight_bytes = 6 * width * hidden
    w_g, w_u, w_d = pl.pallas_call(
        fetch_kernel,
        out_shape=[pltpu.VMEM(w.shape[2:], BF16) for w in (w_gate, w_up, w_down)],
        in_specs=[pl.BlockSpec(memory_space=pltpu.HBM)] * 3,
        out_specs=[pl.BlockSpec(memory_space=pltpu.VMEM)] * 3,
        scratch_shapes=[pltpu.SemaphoreType.DMA((3,))],
        compiler_params=pltpu.CompilerParams(vmem_limit_bytes=VMEM_LIMIT),
        cost_estimate=pl.CostEstimate(flops=0, bytes_accessed=2 * weight_bytes, transcendentals=0),
    )(*[in_hbm(w[0, 0]) for w in (w_gate, w_up, w_down)])
    routes_f, gates_f, routes_b, gates_b = [
        jnp.swapaxes(a[0], 0, 1)
        for a in (routes_forward, gates_forward, routes_backward, gates_backward)
    ]
    spare = -(-4 * topk // held) * LANES
    moved, saved = pl.pallas_call(
        pack_kernel,
        out_shape=[
            jax.ShapeDtypeStruct((2 * held, width), BF16),
            jax.ShapeDtypeStruct((held, width + spare), BF16),
        ],
        in_specs=[pl.BlockSpec(memory_space=pltpu.HBM)] * 7,
        out_specs=[pl.BlockSpec(memory_space=pltpu.VMEM)] * 2,
        scratch_shapes=[pltpu.VMEM(a.shape, a.dtype) for a in (routes_f, gates_f, routes_b, gates_b)]
        + [pltpu.SemaphoreType.DMA((7,))],
        compiler_params=pltpu.CompilerParams(vmem_limit_bytes=VMEM_LIMIT),
        cost_estimate=pl.CostEstimate(flops=0, bytes_accessed=12 * held * width, transcendentals=0),
    )(
        *[in_hbm(a[0]) for a in (carry_forward, carry_cotangent, saved_input)],
        *[in_hbm(a) for a in (routes_f, gates_f, routes_b, gates_b)],
    )
    moved_all = [onward(moved, 2 * d) for d in range(groups)]
    moved_all = [onward(moved, 2 * d) for d in range(groups)]
    saved_all = [saved] + [swap(saved, "expert", 2 * d) for d in range(1, groups)]
    saved_all = saved_all + [swap(x, "expert", 1) for x in saved_all]
    moved_all[0], w_g, w_u, w_d = lax.optimization_barrier((moved_all[0], w_g, w_u, w_d))
    moved_all[1], w_g = lax.optimization_barrier((moved_all[1], w_g))
    w_g, w_u, w_d = in_vmem(w_g), in_vmem(w_u), in_vmem(w_d)
    moved_swap = []
    for x in moved_all:
        if moved_swap:
            x, *_ = lax.optimization_barrier((x, moved_swap[-1], *saved_all))
        moved_swap.append(swap(x, "expert", 1))
    moved_all = moved_all + moved_swap
    part_f, part_b, slot = kernel_call(
        functools.partial(up_kernel, groups, topk, rows, capacity, slot_rows),
        (
            jax.ShapeDtypeStruct((rows, 2 * hidden), BF16),
            jax.ShapeDtypeStruct((rows, 3 * hidden), BF16),
            jax.ShapeDtypeStruct((peers * slot_rows, 2 * rows), BF16),
        ),
        10 * rows * width * hidden,
        weight_bytes,
    )(*moved_all, *saved_all, w_g, w_u, w_d)
    bits = [1 << i for i in range(lax.axis_size("dp").bit_length() - 1)]
    last = bits[-1]
    for up, down in zip(bits, bits[::-1]):
        came_f = mixed(part_f, up, down)
        came_b = mixed(part_b, up, down)
        if up == last:
            break
        part_f = (part_f.astype(F32) + came_f.astype(F32)).astype(BF16)
        part_b = (part_b.astype(F32) + came_b.astype(F32)).astype(BF16)
    grad = kernel_call(
        grad_kernel,
        jax.ShapeDtypeStruct((rows, width), BF16),
        4 * rows * width * hidden,
        4 * width * hidden,
    )(part_b, came_b, w_g, w_u)
    own, other = kernel_call(
        functools.partial(down_kernel, groups),
        [jax.ShapeDtypeStruct((groups, slot_rows, width), BF16)] * 2,
        2 * rows * width * hidden,
        2 * width * hidden,
    )(part_f, came_f, grad, slot, w_d)
    other = swap(other, "expert", 1)
    came = []
    for d in range(1, groups):
        halves = (own[d].astype(F32) + other[d].astype(F32)).astype(BF16)
        came.append(swap(halves, "expert", 2 * d))
    noted = (routes_f, gates_f, routes_b, gates_b)
    *noted, _ = lax.optimization_barrier((*noted, slot))
    home = kernel_call(
        functools.partial(home_kernel, topk, capacity),
        jax.ShapeDtypeStruct((groups, 2 * held, slot_rows), BF16),
        0,
        8 * groups * slot_rows * held,
    )(*noted)
    result_f, result_b = kernel_call(
        functools.partial(final_kernel, groups),
        (
            jax.ShapeDtypeStruct((held, width), BF16),
            jax.ShapeDtypeStruct((held, width), BF16),
        ),
        0,
        20 * held * width,
    )(moved_all[0], home, own, other, *came)
    return (result_f[None], result_b[None])


def solution(mesh):
    placed = (
        P("pipe", "expert", "dp"),
        P("pipe", "expert", "dp"),
        P("pipe", "expert", "dp"),
        P("pipe", "expert", None),
        P("pipe", "expert", None),
        P("pipe", "expert", None),
        P("pipe", "expert", None),
        P("pipe", "expert", "dp", None),
        P("pipe", "expert", "dp", None),
        P("pipe", "expert", None, "dp"),
    )
    return jax.shard_map(
        local,
        mesh=mesh,
        in_specs=placed,
        out_specs=(P("pipe", "expert", "dp"), P("pipe", "expert", "dp")),
        check_vma=False,
    )
```
